128 devices in a mesh: band: 16 (over x, y), chan: 8 (over z, core).
Axes of the slice: x: 4, y: 4, z: 4, core: 2. Of those that a mesh axis runs over, the one named last changes fastest.
Arguments:
- analysed_fields: float32 [227, 32, 1024], P(None, 'band'), may hold values from -6 to 6
- prediction_adjoint_seed: float32 [227, 32, 1024], P(None, 'band'), may hold values from -6 to 6
- encoder_kernel_matrix: bfloat16 [512, 227, 3, 3], P('chan'), may hold values from -0.125 to 0.125
- hidden_offset_term: float32 [512], P('chan'), may hold values from -1 to 1
- decoder_kernel_matrix: bfloat16 [227, 512, 3, 3], P(None, 'chan'), may hold values from -0.09375 to 0.09375
- measurement_wanted_positions: int32 [16, 8, 16, 256], P('band', 'chan'), may hold values from 0 to 32767
- measurement_active_total: int32 [16, 8, 16], P('band', 'chan'), may hold values from 1 to 256, as said below
- measurement_linear_operator: bfloat16 [16, 8, 227, 16, 256], P('band', 'chan'), may hold values from -0.375 to 0.375
Outputs:
- analysis_sensitivity: float32 [227, 32, 1024], P(None, 'band', 'chan')
- obs_impact: float32 [16, 8, 16, 256], P('band', 'chan')
The draws below stay inside these ranges and needn't reach their ends.
Inputs may be any that keep to these rules, and one draw needn't show every extreme that they name: Live slots of each row are the first measurement_active_total of them; 256 is reached in every draw. `measurement_wanted_positions`: position inside target band k on a grid refined 4 times in both directions: fine_row * 1024 * 4 + fine_lon. Slots past the count hold positions as well.
All inputs are finite; a program needn't handle non-finite values.
Results may differ from the reference program's by a relative error of at most 0.015.
Values may be sent and summed in bfloat16 or wider, within the bound.
A program may use at most 128 MiB of HBM per device.

```python
import jax
import jax.numpy as jnp
from jax import lax

PHYSICAL_FIELDS = 227
LATENT = 512
ROWS_DEV = 2
ZONAL_POINTS = 1024
CAP = 256
SUBCELLS = 4
MERIDIAN_LINES = 32
N_BAND = 16
N_CHAN = 8


def draw_measurement_active_total(key, part):
    key = jax.random.fold_in(key, 7)
    key_base, key_level, key_source, key_target = jax.random.split(key, 4)
    level = jax.random.randint(key_level, (1, 1, N_BAND), 1, 5)
    reduction = jax.random.randint(key_base, (N_BAND, N_CHAN, N_BAND), 0, CAP // 4)
    counts = jnp.maximum(1, CAP * level // 4 - reduction)
    source = jax.random.randint(key_source, (), 0, N_BAND)
    target = jax.random.randint(key_target, (), 0, N_BAND)
    counts = counts.at[source, 0, target].set(CAP)
    return counts.astype(jnp.int32)


def with_ends(array, stream_key, least, largest):
    index_at = [jax.random.randint(jax.random.fold_in(stream_key, axis), (), 0, length) for axis, length in enumerate(array.shape)]
    longest = array.shape.index(max(array.shape))
    beside = index_at[:longest] + [(index_at[longest] + 1) % array.shape[longest]] + index_at[longest + 1:]
    return array.at[tuple(index_at)].set(least).at[tuple(beside)].set(largest)


def steps_of(own_key, shape, cuts, least, top_value):
    def one(position, shards_of):
        draws = jax.random.uniform(jax.random.fold_in(jax.random.fold_in(own_key, 6), position), (shards_of,), jnp.float32, least / len(cuts), top_value / len(cuts))
        return jnp.repeat(jnp.exp(draws), shape[position] // shards_of).reshape((-1,) + (1,) * (len(shape) - position - 1))

    loudness = one(*cuts[0])
    for cut in cuts[1:]:
        loudness = loudness * one(*cut)
    return loudness


def bell_draw(rng, dims, width, most, cuts=(), kind=jnp.bfloat16):
    entries = width * jax.random.normal(rng, dims, jnp.float32)
    if cuts:
        entries = entries * steps_of(rng, dims, cuts, -0.22, 0.18)
    return jnp.clip(entries, -most, most).astype(kind)


def setup_inputs(seed: int = 0) -> dict:
    seeds = jax.random.split(jax.random.key(seed), 9)
    return {
        "analysed_fields": bell_draw(seeds[0], (PHYSICAL_FIELDS, MERIDIAN_LINES, ZONAL_POINTS), 1.0, 6.0, ((1, 16),), jnp.float32),
        "prediction_adjoint_seed": bell_draw(seeds[1], (PHYSICAL_FIELDS, MERIDIAN_LINES, ZONAL_POINTS), 1.0, 6.0, ((1, 16),), jnp.float32),
        "encoder_kernel_matrix": bell_draw(seeds[2], (LATENT, PHYSICAL_FIELDS, 3, 3), (PHYSICAL_FIELDS * 9) ** -0.5, 0.125, ((0, 8),)),
        "hidden_offset_term": jnp.clip(jax.random.uniform(seeds[3], (LATENT,), jnp.float32, -1.0, 1.0) * steps_of(seeds[3], (LATENT,), ((0, 8),), -0.4, 0.0), -1.0, 1.0),
        "decoder_kernel_matrix": bell_draw(seeds[4], (PHYSICAL_FIELDS, LATENT, 3, 3), (LATENT * 9) ** -0.5, 0.09375, ((1, 8),)),
        "measurement_wanted_positions": with_ends(jax.random.randint(seeds[5], (N_BAND, N_CHAN, N_BAND, CAP), 0, ROWS_DEV * SUBCELLS * ZONAL_POINTS * SUBCELLS), jax.random.fold_in(seeds[5], 1), 0, (ROWS_DEV * SUBCELLS * ZONAL_POINTS * SUBCELLS) - 1).astype(jnp.int32),
        "measurement_active_total": draw_measurement_active_total(jax.random.fold_in(seeds[8], 71), 0),
        "measurement_linear_operator": bell_draw(seeds[7], (N_BAND, N_CHAN, PHYSICAL_FIELDS, N_BAND, CAP), PHYSICAL_FIELDS ** -0.5, 0.375, ((0, 16), (1, 8))),
    }


def convolve(values, kernel):
    padded = jnp.pad(values.astype(jnp.float32), ((0, 0), (1, 1), (0, 0)))
    wrapped = jnp.concatenate([padded[:, :, -1:], padded, padded[:, :, :1]], axis=2)
    result = lax.conv_general_dilated(wrapped[None], kernel.astype(jnp.float32), (1, 1), "VALID", dimension_numbers=("NCHW", "OIHW", "NCHW"), precision=lax.Precision.HIGHEST)
    return result[0]


def grouped(values, kernel):
    group_width = values.shape[0] // N_CHAN
    summed = jnp.zeros((kernel.shape[0],) + values.shape[1:], jnp.float32)
    for group_index in range(N_CHAN):
        bottom = group_index * group_width
        partial_value = convolve(values[bottom:bottom + group_width], kernel[:, bottom:bottom + group_width])
        summed = summed + lax.optimization_barrier(partial_value.astype(jnp.bfloat16)).astype(jnp.float32)
    return summed


def flipped(kernel):
    return jnp.swapaxes(kernel, 0, 1)[:, :, ::-1, ::-1]


def silu_slope(preact):
    logistic = jax.nn.sigmoid(preact)
    return logistic * (1.0 + preact * (1.0 - logistic))


def interpolate(flat, positions, first_row, span):
    fine_row = positions // (span * SUBCELLS)
    fine_lon = positions % (span * SUBCELLS)
    north = first_row + fine_row // SUBCELLS
    west = fine_lon // SUBCELLS
    east = (west + 1) % span
    row_frac = (fine_row % SUBCELLS).astype(jnp.float32) / SUBCELLS
    lon_frac = (fine_lon % SUBCELLS).astype(jnp.float32) / SUBCELLS
    corner_nw = jnp.take(flat, (north * span + west).astype(jnp.int32), axis=1)
    corner_ne = jnp.take(flat, (north * span + east).astype(jnp.int32), axis=1)
    corner_sw = jnp.take(flat, ((north + 1) * span + west).astype(jnp.int32), axis=1)
    corner_se = jnp.take(flat, ((north + 1) * span + east).astype(jnp.int32), axis=1)
    mixed = (1.0 - row_frac) * (1.0 - lon_frac) * corner_nw + (1.0 - row_frac) * lon_frac * corner_ne + row_frac * (1.0 - lon_frac) * corner_sw + row_frac * lon_frac * corner_se
    return mixed.astype(jnp.bfloat16)


def reference(analysed_fields, prediction_adjoint_seed, encoder_kernel_matrix, hidden_offset_term, decoder_kernel_matrix, measurement_wanted_positions, measurement_active_total, measurement_linear_operator):
    bias = hidden_offset_term[:, None, None]
    first_pre = convolve(analysed_fields.astype(jnp.bfloat16), encoder_kernel_matrix) + bias
    first_hidden = (first_pre * jax.nn.sigmoid(first_pre)).astype(jnp.bfloat16)
    second_state = analysed_fields + grouped(first_hidden, decoder_kernel_matrix)
    second_pre = convolve(second_state.astype(jnp.bfloat16), encoder_kernel_matrix) + bias
    out_flip = flipped(decoder_kernel_matrix)
    in_flip = flipped(encoder_kernel_matrix)
    derivative_mapping = prediction_adjoint_seed
    for preact in (second_pre, first_pre):
        latent_grad = convolve(derivative_mapping.astype(jnp.bfloat16), out_flip)
        slope = (latent_grad * silu_slope(preact)).astype(jnp.bfloat16)
        derivative_mapping = derivative_mapping + grouped(slope, in_flip)
    grid = jnp.concatenate([derivative_mapping, jnp.zeros((PHYSICAL_FIELDS, 1, ZONAL_POINTS), jnp.float32)], axis=1).reshape(PHYSICAL_FIELDS, -1)
    band_first = (jnp.arange(N_BAND, dtype=jnp.int32) * ROWS_DEV)[None, :, None]

    def per_owner(inputs):
        positions, jacobian, counts = inputs
        columns = interpolate(grid, positions, band_first, ZONAL_POINTS)
        impact = jnp.einsum("cjks,jcks->jks", columns.astype(jnp.float32), jacobian.astype(jnp.float32), precision=lax.Precision.HIGHEST)
        live = jnp.arange(CAP, dtype=jnp.int32)[None, None, :] < counts[:, :, None]
        return jnp.where(live, impact, jnp.float32(0.0))

    obs_impact = lax.map(per_owner, (measurement_wanted_positions, measurement_linear_operator, measurement_active_total))
    return derivative_mapping, obs_impact
```

```python
import jax
import jax.numpy as jnp
from jax import lax
from jax.experimental import pallas as pl
from jax.experimental.pallas import tpu as pltpu
from jax.sharding import PartitionSpec as P

MESH = pl.DeviceIdType.MESH
F32 = jnp.float32
BF16 = jnp.bfloat16

FIELDS = 227
CH = 256
NB = 16
NZ = 4
ROWS = 32
LON = 1024
OWN = 128
EDGE = 8
W = OWN + 2 * EDGE
JC = 240
CAP = 256
LATENT = 512


def dot(a, b):
    return lax.dot_general(a, b, (((1,), (0,)), ((), ())), preferred_element_type=F32)


def dot_nt(a, b):
    return lax.dot_general(a, b, (((1,), (1,)), ((), ())), preferred_element_type=F32)


def slope(u):
    s = jax.nn.sigmoid(u)
    return s * (1.0 + u * (1.0 - s))


def kernel(
    w_ref, x_ref, seed_ref, op_ref, pos_ref, sens_ref, imp_ref,
    wts, xin, sdin, xb, sdb, pre1, lat2, sh, hb, s2, s2b, sb, mid, midin, midb,
    gt, opr, posr, tent, impbuf, impin,
    wsend, wrecv, gsend, grecv, xsend, xrecv, ssend, srecv, msend, mrecv,
    psend, precv, osend, orecv, osem, isend, irecv,
):
    band = lax.axis_index("band")
    chan = lax.axis_index("chan")
    z = chan // 2
    core = chan % 2
    sib = (band, 2 * z + (1 - core))
    zp = (band, 2 * lax.rem(z + 1, NZ) + core)
    zm = (band, 2 * lax.rem(z + NZ - 1, NZ) + core)

    def at_band(d):
        return (lax.rem(band + (d + NB), NB), chan)

    barrier = pltpu.get_barrier_semaphore()
    for d in range(1, NB):
        pl.semaphore_signal(barrier, inc=1, device_id=at_band(d), device_id_type=MESH)
    for dev in (sib, zp, zm):
        pl.semaphore_signal(barrier, inc=1, device_id=dev, device_id_type=MESH)
    pl.semaphore_wait(barrier, NB - 1 + 3)

    def copy(src, dst, ss, rs, dev):
        return pltpu.make_async_remote_copy(
            src_ref=src, dst_ref=dst, send_sem=ss, recv_sem=rs, device_id=dev, device_id_type=MESH
        )

    def gather(region, half, ss, rs):
        return [
            copy(region(0), region(0), ss.at[0], rs.at[0], sib),
            copy(region(0), region(1), ss.at[1], rs.at[1], zp),
            copy(region(0), region(2), ss.at[2], rs.at[2], zm),
            copy(region(1), region(1), ss.at[3], rs.at[3], sib),
            copy(region(2), region(2), ss.at[4], rs.at[4], sib),
            copy(half(1, 0), half(3, 0), ss.at[5], rs.at[5], zp),
            copy(half(2, 1), half(3, 1), ss.at[6], rs.at[6], zm),
            copy(half(3, 0), half(3, 0), ss.at[7], rs.at[7], sib),
            copy(half(3, 1), half(3, 1), ss.at[8], rs.at[8], sib),
        ]

    lrow = pl.multiple_of(core * 64, 64)
    wcopies = gather(
        lambda q: wts.at[:, q, pl.ds(lrow, 64), :],
        lambda q, h: wts.at[pl.ds(9 * h, 9), q, pl.ds(lrow, 64), :],
        wsend, wrecv,
    )
    wts[:, 0, pl.ds(lrow, 64), :] = w_ref[...]
    for c in wcopies[:3]:
        c.start()

    xin[2 * 288:3 * 288, :] = x_ref[...].astype(BF16)
    sdin[288:2 * 288, :] = seed_ref[...].astype(BF16)
    xcopies, scopies = [], []
    for n, d in enumerate((1, -1, 2, -2)):
        xcopies.append(copy(
            xin.at[pl.ds(576, 288), :], xin.at[pl.ds((2 - d) * 288, 288), :], xsend.at[n], xrecv.at[n], at_band(d)))
    for n, d in enumerate((1, -1)):
        scopies.append(copy(
            sdin.at[pl.ds(288, 288), :], sdin.at[pl.ds((1 - d) * 288, 288), :], ssend.at[n], srecv.at[n], at_band(d)))
    for c in xcopies + scopies:
        c.start()

    def pcopy(d):
        return copy(pos_ref.at[lax.rem(band + d, NB)], posr.at[d], psend.at[d], precv.at[d], at_band(d))

    def ocopy(d):
        return copy(op_ref.at[lax.rem(band + d, NB)], opr.at[d], osend.at[d], orecv.at[d], at_band(d))

    posr[0] = pos_ref[band]
    own_op = pltpu.make_async_copy(op_ref.at[band], opr.at[0], osem)
    own_op.start()
    for d in range(1, NB):
        pcopy(d).start()
    for d in range(1, NB):
        ocopy(d).start()

    def shift3(dst, rows, width, first, flip):
        for r in range(rows):
            at = 2 * band + (first + r)
            live = jnp.logical_and(at >= 0, at < ROWS)
            for b in range(3):
                v = sh[8 + r * W + b - 1:8 + r * W + b - 1 + W, :width]
                lane = (2 - b if flip else b) * width
                dst[r * W:(r + 1) * W, lane:lane + width] = jnp.where(live, v, 0.0).astype(BF16)

    def rows_of(ref, base, n, width):
        return jnp.concatenate([ref[pl.ds(pl.multiple_of(base + a * W, 16), n), :width] for a in range(3)], axis=1)

    def taps(first, flip, q, nq, axis):
        parts = []
        for a in range(3):
            k = first + 3 * (2 - a if flip else a)
            if axis == 0:
                parts.append(wts[k:k + 3, q:q + nq].reshape(3 * nq * 128, CH))
            else:
                parts += [wts[k + b, q:q + nq].reshape(nq * 128, CH) for b in range(3)]
        return jnp.concatenate(parts, axis=axis)

    for c in xcopies + scopies:
        c.wait_recv()
    sh[8:8 + 10 * W, :CH] = xin[...].astype(F32)
    shift3(xb, 10, CH, -4, False)
    sh[8:8 + 6 * W, :CH] = sdin[...].astype(F32)
    shift3(sdb, 6, CH, -2, True)
    s2[0:288, :] = xin[288:576, :].astype(F32)
    s2[288:576, :] = x_ref[...]
    s2[576:864, :] = xin[864:1152, :].astype(F32)

    def first_half(q, nq):
        width, off = nq * 128, q * 128

        def conv1(t, _):
            base = pl.multiple_of(t * 288, 16)
            p = dot_nt(rows_of(xb, base, 288, 3 * CH), taps(0, False, q, nq, 1))
            pre1[pl.ds(base, 288), off:off + width] = p
            sh[pl.ds(pl.multiple_of(base + 8, 8), 288), :width] = p * jax.nn.sigmoid(p)
            return 0

        lax.fori_loop(0, 4, conv1, 0)
        shift3(hb, 8, width, -3, False)

        def conv2(t, _):
            base = pl.multiple_of(t * 288, 16)
            s2[pl.ds(base, 288), :] += dot(rows_of(hb, base, 288, 3 * width), taps(9, False, q, nq, 0))
            return 0

        lax.fori_loop(0, 3, conv2, 0)

        def back(t, _):
            base = pl.multiple_of(t * 288, 16)
            lat2[pl.ds(base, 288), off:off + width] = dot_nt(
                rows_of(sdb, base, 288, 3 * CH), taps(9, True, q, nq, 1))
            return 0

        lax.fori_loop(0, 2, back, 0)

    wcopies[0].wait_recv()
    first_half(0, 1)

    for d in range(1, NB):
        pcopy(d).wait_recv()

    def build(d, _):
        lon = (posr[d] & (4 * LON - 1)).astype(F32) * 0.25
        for q, dz in enumerate((0, NZ - 1, 1, 2)):
            at = lax.rem(z + dz, NZ) * 256
            west = (lax.broadcasted_iota(jnp.int32, (256, CAP), 0) + at).astype(F32)
            gap = jnp.abs(west - lon)
            gap = jnp.minimum(gap, LON - gap)
            tent[d, q * 256:(q + 1) * 256, :] = jnp.maximum(1.0 - gap, 0.0).astype(BF16)
        return 0

    lax.fori_loop(0, NB, build, 0)

    wcopies[1].wait_recv()
    wcopies[5].start()
    wcopies[3].start()
    wcopies[2].wait_recv()
    wcopies[6].start()
    wcopies[4].start()
    wcopies[3].wait_recv()
    wcopies[4].wait_recv()
    first_half(1, 2)
    wcopies[5].wait_recv()
    wcopies[7].start()
    wcopies[6].wait_recv()
    wcopies[8].start()
    wcopies[7].wait_recv()
    wcopies[8].wait_recv()
    first_half(3, 1)

    sh[8:8 + 6 * W, :CH] = s2[...]
    shift3(s2b, 6, CH, -2, False)

    def second(t, _):
        base = pl.multiple_of(t * 288, 16)
        p = dot_nt(rows_of(s2b, base, 288, 3 * CH), taps(0, False, 0, 4, 1))
        sh[pl.ds(pl.multiple_of(base + 8, 8), 288), :] = lat2[pl.ds(base, 288), :] * slope(p)
        return 0

    lax.fori_loop(0, 2, second, 0)
    shift3(sb, 4, LATENT, -1, True)
    mid[...] = seed_ref[...] + dot(rows_of(sb, 0, 288, 3 * LATENT), taps(0, True, 0, 4, 0))
    midin[288:576, :] = mid[...].astype(BF16)
    mcopies = [
        copy(midin.at[pl.ds(288, 288), :], midin.at[pl.ds(0, 288), :], msend.at[0], mrecv.at[0], at_band(1)),
        copy(midin.at[pl.ds(288, 288), :], midin.at[pl.ds(576, 288), :], msend.at[1], mrecv.at[1], at_band(-1)),
        copy(midin.at[pl.ds(288, W), :], midin.at[pl.ds(864, W), :], msend.at[2], mrecv.at[2], at_band(-2)),
    ]
    for c in mcopies:
        c.start()
    for c in mcopies:
        c.wait_recv()

    sh[8:8 + 7 * W, :CH] = midin[...].astype(F32)
    shift3(midb, 7, CH, -2, True)

    def first(t, _):
        base = pl.multiple_of(t * W, 16)
        v = dot_nt(rows_of(midb, base, W, 3 * CH), taps(9, True, 0, 4, 1))
        sh[pl.ds(pl.multiple_of(base + 8, 8), W), :] = v * slope(pre1[pl.ds(pl.multiple_of(base + 288, 16), W), :])
        return 0

    lax.fori_loop(0, 5, first, 0)
    shift3(sb, 5, LATENT, -1, True)
    for r in range(3):
        start = mid[r * W:(r + 1) * W, :] if r < 2 else midin[4 * W:5 * W, :].astype(F32)
        g = start + dot(rows_of(sb, r * W, W, 3 * LATENT), taps(0, True, 0, 4, 0))
        g = jnp.transpose(g[EDGE:EDGE + OWN, :])
        if r < 2:
            sens_ref[r] = g
        else:
            g = jnp.where(band < NB - 1, g, 0.0)
        gt[core, r * CH:(r + 1) * CH, :] = g.astype(BF16)

    gcopies = gather(
        lambda q: gt.at[2 * q + core],
        lambda q, h: gt.at[2 * q + core, pl.ds(384 * h, 384), :],
        gsend, grecv,
    )
    for c in gcopies[:3]:
        c.start()
    gcopies[1].wait_recv()
    gcopies[5].start()
    gcopies[3].start()
    gcopies[2].wait_recv()
    gcopies[6].start()
    gcopies[4].start()
    gcopies[5].wait_recv()
    gcopies[7].start()
    gcopies[6].wait_recv()
    gcopies[8].start()
    for n in (0, 3, 4, 7, 8):
        gcopies[n].wait_recv()

    own_op.wait()
    for d in range(1, NB):
        ocopy(d).wait_recv()

    def icopy(d):
        return copy(impbuf.at[d], impin.at[band], isend.at[d], irecv.at[d], at_band(-d))

    def observe(d, _):
        m = dot(jnp.concatenate([gt[n] for n in range(8)], axis=1), tent[d])
        row = (posr[d] // (4 * LON)).astype(F32) * 0.25
        col = jnp.maximum(1.0 - row, 0.0) * m[0:JC]
        col += jnp.maximum(1.0 - jnp.abs(row - 1.0), 0.0) * m[CH:CH + JC]
        col += jnp.maximum(row - 1.0, 0.0) * m[2 * CH:2 * CH + JC]
        impbuf[d] = jnp.sum(col * opr[d].astype(F32), axis=0, keepdims=True)
        return 0

    for d in range(NB):
        observe(d, 0)
        if d > 0:
            icopy(d).start()
    impin[band] = impbuf[0]
    for d in range(1, NB):
        pltpu.make_async_remote_copy(
            src_ref=impbuf.at[d], dst_ref=impin.at[lax.rem(band + d, NB)], send_sem=isend.at[d],
            recv_sem=irecv.at[d], device_id=at_band(-d), device_id_type=MESH).wait_recv()
    imp_ref[...] = impin[...]
    for c in wcopies + xcopies + scopies + mcopies + gcopies:
        c.wait_send()
    for d in range(1, NB):
        pcopy(d).wait_send()
        ocopy(d).wait_send()
        icopy(d).wait_send()


def fused(w, x, seed, op, pos):
    def vm(shape, dtype):
        return pltpu.VMEM(shape, dtype)

    dma = pltpu.SemaphoreType.DMA
    return pl.pallas_call(
        kernel,
        out_shape=(
            jax.ShapeDtypeStruct((2, CH, OWN), F32),
            jax.ShapeDtypeStruct((NB, 1, CAP), F32),
        ),
        in_specs=[pl.BlockSpec(memory_space=pltpu.VMEM)] * 3
        + [pl.BlockSpec(memory_space=pl.ANY), pl.BlockSpec(memory_space=pltpu.VMEM)],
        out_specs=(pl.BlockSpec(memory_space=pltpu.VMEM),) * 2,
        scratch_shapes=[
            vm((18, 4, 128, CH), BF16),
            vm((10 * W, CH), BF16),
            vm((6 * W, CH), BF16),
            vm((10 * W, 3 * CH), BF16),
            vm((6 * W, 3 * CH), BF16),
            vm((8 * W, LATENT), F32),
            vm((4 * W, LATENT), F32),
            vm((10 * W + 16, LATENT), F32),
            vm((8 * W, 3 * 256), BF16),
            vm((6 * W, CH), F32),
            vm((6 * W, 3 * CH), BF16),
            vm((5 * W, 3 * LATENT), BF16),
            vm((2 * W, CH), F32),
            vm((7 * W, CH), BF16),
            vm((7 * W, 3 * CH), BF16),
            vm((8, 3 * CH, OWN), BF16),
            vm((NB, JC, CAP), BF16),
            vm((NB, 1, CAP), jnp.int32),
            vm((NB, LON, CAP), BF16),
            vm((NB, 1, CAP), F32),
            vm((NB, 1, CAP), F32),
            dma((9,)), dma((9,)), dma((9,)), dma((9,)),
            dma((4,)), dma((4,)), dma((2,)), dma((2,)), dma((3,)), dma((3,)),
            dma((NB,)), dma((NB,)), dma((NB,)), dma((NB,)), dma, dma((NB,)), dma((NB,)),
        ],
        compiler_params=pltpu.CompilerParams(
            collective_id=0, has_side_effects=True, vmem_limit_bytes=60 * 1024 * 1024
        ),
    )(w, x, seed, op, pos)


def window(state, start, fill):
    around = jnp.concatenate([state[:, :, -EDGE:], state, state[:, :, :EDGE]], axis=2)
    part = lax.dynamic_slice_in_dim(around, start, W, 2)
    part = jnp.transpose(part, (1, 2, 0)).reshape(2 * W, FIELDS)
    ones = jnp.full((2 * W, 3), fill, F32)
    return jnp.concatenate([part, ones, jnp.zeros((2 * W, CH - FIELDS - 3), F32)], axis=1)


def local(
    analysed_fields,
    prediction_adjoint_seed,
    encoder_kernel_matrix,
    hidden_offset_term,
    decoder_kernel_matrix,
    measurement_wanted_positions,
    measurement_active_total,
    measurement_linear_operator,
):
    start = lax.axis_index("chan") * OWN
    enc = jnp.transpose(encoder_kernel_matrix, (2, 3, 0, 1)).reshape(9, 64, FIELDS)
    dec = jnp.transpose(decoder_kernel_matrix, (2, 3, 1, 0)).reshape(9, 64, FIELDS)
    high = lax.reduce_precision(hidden_offset_term, 8, 7)
    middle = lax.reduce_precision(hidden_offset_term - high, 8, 7)
    low = hidden_offset_term - high - middle
    bias = jnp.stack([high, middle, low], axis=1)[None].astype(BF16)
    bias = jnp.pad(bias, ((4, 13), (0, 0), (FIELDS, CH - FIELDS - 3)))
    w = jnp.pad(jnp.concatenate([enc, dec], axis=0), ((0, 0), (0, 0), (0, CH - FIELDS))) + bias
    op = jnp.pad(jnp.transpose(measurement_linear_operator[0, 0], (1, 0, 2)), ((0, 0), (0, JC - FIELDS), (0, 0)))
    pos = measurement_wanted_positions[0, 0][:, None, :]
    sens, imp = fused(
        w, window(analysed_fields, start, 1.0), window(prediction_adjoint_seed, start, 0.0), op, pos)
    sensitivity = jnp.transpose(sens[:, :FIELDS, :], (1, 0, 2))
    live = jnp.arange(CAP, dtype=jnp.int32)[None, :] < measurement_active_total[0, 0][:, None]
    impact = jnp.where(live, imp[:, 0, :], jnp.float32(0.0))
    return (sensitivity, impact[None, None])


def solution(mesh):
    in_specs = (
        P(None, "band", None),
        P(None, "band", None),
        P("chan", None, None, None),
        P("chan"),
        P(None, "chan", None, None),
        P("band", "chan", None, None),
        P("band", "chan", None),
        P("band", "chan", None, None, None),
    )
    out_specs = (P(None, "band", "chan"), P("band", "chan", None, None))
    return jax.shard_map(local, mesh=mesh, in_specs=in_specs, out_specs=out_specs, check_vma=False)
```

```python
import jax
import jax.numpy as jnp
from jax import lax
from jax.experimental import pallas as pl
from jax.experimental.pallas import tpu as pltpu
from jax.sharding import PartitionSpec as P

MESH = pl.DeviceIdType.MESH
F32 = jnp.float32
BF16 = jnp.bfloat16

FIELDS = 227
CH = 256
NB = 16
NZ = 4
ROWS = 32
LON = 1024
OWN = 128
EDGE = 8
W = OWN + 2 * EDGE
JC = 240
CAP = 256
LATENT = 512
OP_FIRST = 8


def dot(a, b):
    return lax.dot_general(a, b, (((1,), (0,)), ((), ())), preferred_element_type=F32)


def dot_nt(a, b):
    return lax.dot_general(a, b, (((1,), (1,)), ((), ())), preferred_element_type=F32)


def slope(u):
    s = jax.nn.sigmoid(u)
    return s * (1.0 + u * (1.0 - s))


def kernel(
    enc_ref, dec_ref, bias_ref, x_ref, seed_ref, op_ref, pos_ref, sens_ref, imp_ref,
    wts, raw, x, seed, xin, sdin, stin, midin, xb, sdb, pre1, lat2, sh, hb, s2, sb, mid,
    gt, opr, posb, posr, tent, part, impbuf, impin,
    rsem, wsend, wrecv, gsend, grecv, hsend, hrecv, xsend, xrecv,
    psend, precv, osend, orecv, osem, isend, irecv,
):
    band = lax.axis_index("band")
    chan = lax.axis_index("chan")
    z = chan // 2
    core = chan % 2
    sib = (band, 2 * z + (1 - core))
    zp = (band, 2 * lax.rem(z + 1, NZ) + core)
    zm = (band, 2 * lax.rem(z + NZ - 1, NZ) + core)

    def at_band(d):
        return (lax.rem(band + (d + NB), NB), chan)

    fetches = []
    for n, ref in enumerate((x_ref, seed_ref)):
        for t in range(3):
            block = pl.ds(pl.multiple_of(lax.rem(chan + (t + 7), 8) * OWN, OWN), OWN)
            fetches.append(pltpu.make_async_copy(
                ref.at[:, :, block], raw.at[n, pl.ds(0, FIELDS), :, pl.ds(t * OWN, OWN)], rsem.at[n, t]))
    for c in fetches:
        c.start()

    barrier = pltpu.get_barrier_semaphore()
    for d in range(1, NB):
        pl.semaphore_signal(barrier, inc=1, device_id=at_band(d), device_id_type=MESH)
    for dev in (sib, zp, zm):
        pl.semaphore_signal(barrier, inc=1, device_id=dev, device_id_type=MESH)

    lrow = pl.multiple_of(core * 64, 64)
    for n, ref in enumerate((enc_ref, dec_ref)):
        for k in range(9):
            wts[9 * n + k, 0, pl.ds(lrow, 64), 0:128] = ref[k, :, 0:128]
            rest = jnp.concatenate([ref[k, :, 128:FIELDS], jnp.zeros((64, CH - FIELDS), BF16)], axis=1)
            if n == 0 and k == 4:
                eye = lax.broadcasted_iota(jnp.int32, (64, 64), 0) == lax.broadcasted_iota(jnp.int32, (64, 64), 1)
                bias = jnp.sum(jnp.where(eye, bias_ref[...], 0.0), axis=1, keepdims=True)
                high = bias.astype(BF16).astype(F32)
                middle = (bias - high).astype(BF16).astype(F32)
                low = bias - high - middle
                lane = lax.broadcasted_iota(jnp.int32, (64, 128), 1) + 128
                terms = jnp.where(lane == FIELDS, high, jnp.where(lane == FIELDS + 1, middle, low))
                terms = jnp.where(jnp.logical_and(lane >= FIELDS, lane < FIELDS + 3), terms, 0.0)
                rest = (rest.astype(F32) + terms).astype(BF16)
            wts[9 * n + k, 0, pl.ds(lrow, 64), 128:256] = rest

    pl.semaphore_wait(barrier, NB - 1 + 3)

    def copy(src, dst, ss, rs, dev):
        return pltpu.make_async_remote_copy(
            src_ref=src, dst_ref=dst, send_sem=ss, recv_sem=rs, device_id=dev, device_id_type=MESH
        )

    def gather(region, half, ss, rs):
        return [
            copy(region(0), region(0), ss.at[0], rs.at[0], sib),
            copy(region(0), region(1), ss.at[1], rs.at[1], zp),
            copy(region(0), region(2), ss.at[2], rs.at[2], zm),
            copy(region(1), region(1), ss.at[3], rs.at[3], sib),
            copy(region(2), region(2), ss.at[4], rs.at[4], sib),
            copy(half(1, 0), half(3, 0), ss.at[5], rs.at[5], zp),
            copy(half(2, 1), half(3, 1), ss.at[6], rs.at[6], zm),
            copy(half(3, 0), half(3, 0), ss.at[7], rs.at[7], sib),
            copy(half(3, 1), half(3, 1), ss.at[8], rs.at[8], sib),
        ]

    wcopies = gather(
        lambda q: wts.at[:, q, pl.ds(lrow, 64), :],
        lambda q, h: wts.at[pl.ds(9 * h, 9), q, pl.ds(lrow, 64), :],
        wsend, wrecv,
    )
    for c in wcopies[:3]:
        c.start()

    def exchange(ref, n):
        own = ref.at[pl.ds(288, 288), :]
        return [
            copy(own, ref.at[pl.ds(0, 288), :], xsend.at[n, 0], xrecv.at[n, 0], at_band(1)),
            copy(own, ref.at[pl.ds(576, 288), :], xsend.at[n, 1], xrecv.at[n, 1], at_band(-1)),
        ]

    halos = [exchange(ref, n) for n, ref in enumerate((xin, sdin, stin, midin))]
    for n, (ref, own, fill) in enumerate(((x, xin, 1.0), (seed, sdin, 0.0))):
        for t in range(3):
            fetches[3 * n + t].wait()
        channel = lax.broadcasted_iota(jnp.int32, (CH - 224, 3 * OWN), 0) + 224
        for r in range(2):
            tail = raw[n, 224:CH, r, :]
            tail = jnp.where(channel < FIELDS, tail, jnp.where(channel < FIELDS + 3, fill, 0.0))
            rows = jnp.concatenate([raw[n, 0:224, r, :], tail], axis=0)
            ref[r * W:r * W + EDGE, :] = jnp.transpose(rows[:, 0:OWN])[OWN - EDGE:, :]
            ref[r * W + EDGE:r * W + EDGE + OWN, :] = jnp.transpose(rows[:, OWN:2 * OWN])
            ref[r * W + EDGE + OWN:(r + 1) * W, :] = jnp.transpose(rows[:, 2 * OWN:3 * OWN])[:EDGE, :]
        own[288:576, :] = ref[...].astype(BF16)
        for c in halos[n]:
            c.start()

    def pcopy(d):
        return copy(posb.at[lax.rem(band + d, NB)], posr.at[d], psend.at[d], precv.at[d], at_band(d))

    def ocopy(d):
        return copy(op_ref.at[lax.rem(band + d, NB)], opr.at[d], osend.at[d], orecv.at[d], at_band(d))

    for k in range(NB):
        posb[k] = pos_ref[k:k + 1, :]
    posr[0] = posb[band]
    for d in range(1, NB):
        pcopy(d).start()
    own_op = pltpu.make_async_copy(op_ref.at[band], opr.at[0], osem)
    own_op.start()

    def shift3(dst, rows, width, first, flip):
        for r in range(rows):
            at = 2 * band + (first + r)
            live = jnp.logical_and(at >= 0, at < ROWS)
            for b in range(3):
                v = sh[8 + r * W + b - 1:8 + r * W + b - 1 + W, :width]
                lane = (2 - b if flip else b) * width
                dst[r * W:(r + 1) * W, lane:lane + width] = jnp.where(live, v, 0.0).astype(BF16)

    def spread(dst, ref, flip):
        sh[8:8 + 6 * W, :CH] = ref[...].astype(F32)
        shift3(dst, 6, CH, -2, flip)

    def rows_of(ref, n, width):
        return jnp.concatenate([ref[a * W:a * W + n, :width] for a in range(3)], axis=1)

    def taps(first, flip, lat, axis):
        parts = []
        for a in range(3):
            k = first + 3 * (2 - a if flip else a)
            if axis == 0:
                part_ = wts[k:k + 3, lat]
                parts.append(part_.reshape(part_.shape[0] * part_.shape[1] * part_.shape[2], CH))
            else:
                for b in range(3):
                    part_ = wts[k + b, lat]
                    parts.append(part_.reshape(part_.shape[0] * part_.shape[1], CH))
        return jnp.concatenate(parts, axis=axis)

    for c in halos[0]:
        c.wait_recv()
    spread(xb, xin, False)
    s2[...] = x[...]

    def first_half(q, nq, parts):
        width, off = nq * 128, q * 128
        lat = pl.ds(q, nq)
        if "state" in parts:
            p = dot_nt(rows_of(xb, 4 * W, 3 * CH), taps(0, False, lat, 1))
            pre1[:, off:off + width] = p
            sh[8:8 + 4 * W, :width] = p * jax.nn.sigmoid(p)
            shift3(hb, 4, width, -1, False)
            s2[...] += dot(rows_of(hb, 2 * W, 3 * width), taps(9, False, lat, 0))
        if "seed" in parts:
            lat2[:, off:off + width] = dot_nt(rows_of(sdb, 4 * W, 3 * CH), taps(9, True, lat, 1))

    wcopies[0].wait_recv()
    first_half(0, 1, ("state",))
    for c in halos[1]:
        c.wait_recv()
    spread(sdb, sdin, True)
    for d in range(1, OP_FIRST):
        ocopy(d).start()
    first_half(0, 1, ("seed",))

    for d in range(1, NB):
        pcopy(d).wait_recv()

    def build(d, _):
        lon = (posr[d] & (4 * LON - 1)).astype(F32) * 0.25
        for q, dz in enumerate((0, NZ - 1, 1, 2)):
            at = lax.rem(z + dz, NZ) * 256
            west = (lax.broadcasted_iota(jnp.int32, (256, CAP), 0) + at).astype(F32)
            gap = jnp.abs(west - lon)
            gap = jnp.minimum(gap, LON - gap)
            tent[d, q * 256:(q + 1) * 256, :] = jnp.maximum(1.0 - gap, 0.0).astype(BF16)
        return 0

    lax.fori_loop(0, NB, build, 0)

    wcopies[1].wait_recv()
    wcopies[5].start()
    wcopies[3].start()
    wcopies[2].wait_recv()
    wcopies[6].start()
    wcopies[4].start()
    wcopies[3].wait_recv()
    wcopies[4].wait_recv()
    first_half(1, 2, ("state", "seed"))
    wcopies[5].wait_recv()
    wcopies[7].start()
    wcopies[6].wait_recv()
    wcopies[8].start()
    wcopies[7].wait_recv()
    wcopies[8].wait_recv()
    first_half(3, 1, ("state",))
    stin[288:576, :] = s2[...].astype(BF16)
    for c in halos[2]:
        c.start()
    first_half(3, 1, ("seed",))

    for c in halos[2]:
        c.wait_recv()
    spread(xb, stin, False)

    def second(t, _):
        off = pl.multiple_of(t * 256, 256)
        p = dot_nt(rows_of(xb, 4 * W, 3 * CH), taps(0, False, pl.ds(2 * t, 2), 1))
        sh[8:8 + 4 * W, pl.ds(off, 256)] = lat2[:, pl.ds(off, 256)] * slope(p)
        return 0

    lax.fori_loop(0, 2, second, 0)
    shift3(sb, 4, LATENT, -1, True)
    mid[...] = seed[...] + dot(rows_of(sb, 2 * W, 3 * LATENT), taps(0, True, pl.ds(0, 4), 0))
    midin[288:576, :] = mid[...].astype(BF16)
    for c in halos[3]:
        c.start()
    for c in halos[3]:
        c.wait_recv()
    for d in range(OP_FIRST, NB):
        ocopy(d).start()

    spread(sdb, midin, True)

    def first(t, _):
        off = pl.multiple_of(t * 256, 256)
        v = dot_nt(rows_of(sdb, 4 * W, 3 * CH), taps(9, True, pl.ds(2 * t, 2), 1))
        sh[8:8 + 4 * W, pl.ds(off, 256)] = v * slope(pre1[:, pl.ds(off, 256)])
        return 0

    lax.fori_loop(0, 2, first, 0)
    shift3(sb, 4, LATENT, -1, True)
    mid[...] += dot(rows_of(sb, 2 * W, 3 * LATENT), taps(0, True, pl.ds(0, 4), 0))
    for r in range(2):
        g = jnp.transpose(mid[r * W + EDGE:r * W + EDGE + OWN, :])
        sens_ref[:, r, :] = g[:FIELDS]
        gt[core, r * JC:(r + 1) * JC, :] = g[:JC].astype(BF16)

    below = copy(gt.at[core, pl.ds(0, JC), :], gt.at[core, pl.ds(2 * JC, JC), :], hsend, hrecv, at_band(-1))
    below.start()
    own_rows = gather(
        lambda q: gt.at[2 * q + core, pl.ds(0, 2 * JC), :],
        lambda q, h: gt.at[2 * q + core, pl.ds(JC * h, JC), :],
        gsend.at[0], grecv.at[0],
    )
    next_row = gather(
        lambda q: gt.at[2 * q + core, pl.ds(2 * JC, JC), :],
        lambda q, h: gt.at[2 * q + core, pl.ds(2 * JC + 112 * h, 112 + 16 * h), :],
        gsend.at[1], grecv.at[1],
    )
    for c in own_rows[:3]:
        c.start()
    below.wait_recv()
    gt[core, 2 * JC:3 * JC, :] = jnp.where(band < NB - 1, gt[core, 2 * JC:3 * JC, :].astype(F32), 0.0).astype(BF16)
    for c in next_row[:3]:
        c.start()

    own_rows[0].wait_recv()

    def near(d, _):
        part[d] = dot(jnp.concatenate([gt[n, 0:2 * JC] for n in range(2)], axis=1), tent[d, 0:256])
        return 0

    lax.fori_loop(0, NB, near, 0)

    for g in (own_rows, next_row):
        g[1].wait_recv()
        g[5].start()
        g[3].start()
        g[2].wait_recv()
        g[6].start()
        g[4].start()
    own_rows[3].wait_recv()
    own_rows[4].wait_recv()
    for g in (own_rows, next_row):
        g[5].wait_recv()
        g[7].start()
        g[6].wait_recv()
        g[8].start()

    def beside(d, _):
        part[d] += dot(jnp.concatenate([gt[n, 0:2 * JC] for n in range(2, 6)], axis=1), tent[d, 256:768])
        return 0

    lax.fori_loop(0, NB, beside, 0)

    own_rows[7].wait_recv()
    own_rows[8].wait_recv()
    for n in (0, 3, 4, 7, 8):
        next_row[n].wait_recv()

    def icopy(d):
        return copy(impbuf.at[d], impin.at[band], isend.at[d], irecv.at[d], at_band(-d))

    def observe(d):
        m = part[d] + dot(jnp.concatenate([gt[n, 0:2 * JC] for n in range(6, 8)], axis=1), tent[d, 768:1024])
        m2 = dot(jnp.concatenate([gt[n, 2 * JC:3 * JC] for n in range(8)], axis=1), tent[d])
        row = (posr[d] // (4 * LON)).astype(F32) * 0.25
        col = jnp.maximum(1.0 - row, 0.0) * m[0:JC]
        col += jnp.maximum(1.0 - jnp.abs(row - 1.0), 0.0) * m[JC:2 * JC]
        col += jnp.maximum(row - 1.0, 0.0) * m2
        impbuf[d] = jnp.sum(col * opr[d].astype(F32), axis=0, keepdims=True)

    def answer(d, _):
        ocopy(d).wait_recv()
        observe(d)
        icopy(d).start()
        return 0

    lax.fori_loop(1, NB, answer, 0)
    own_op.wait()
    observe(0)
    impin[band] = impbuf[0]
    for d in range(1, NB):
        copy(impbuf.at[d], impin.at[lax.rem(band + d, NB)], isend.at[d], irecv.at[d], at_band(-d)).wait_recv()
    for k in range(NB):
        imp_ref[k:k + 1, :] = impin[k]
    for c in wcopies + sum(halos, []) + own_rows + next_row + [below]:
        c.wait_send()
    for d in range(1, NB):
        pcopy(d).wait_send()
        ocopy(d).wait_send()
        icopy(d).wait_send()


def fused(enc, dec, bias, x, seed, op, pos):
    def vm(shape, dtype):
        return pltpu.VMEM(shape, dtype)

    vmem, anywhere = pl.BlockSpec(memory_space=pltpu.VMEM), pl.BlockSpec(memory_space=pl.ANY)
    dma = pltpu.SemaphoreType.DMA
    return pl.pallas_call(
        kernel,
        out_shape=(
            jax.ShapeDtypeStruct((FIELDS, 2, OWN), F32),
            jax.ShapeDtypeStruct((NB, CAP), F32),
        ),
        in_specs=[vmem, vmem, vmem, anywhere, anywhere, anywhere, vmem],
        out_specs=(vmem, vmem),
        scratch_shapes=[
            vm((18, 4, 128, CH), BF16),
            vm((2, CH, 2, 3 * OWN), F32),
            vm((2 * W, CH), F32),
            vm((2 * W, CH), F32),
            vm((6 * W, CH), BF16),
            vm((6 * W, CH), BF16),
            vm((6 * W, CH), BF16),
            vm((6 * W, CH), BF16),
            vm((6 * W, 3 * CH), BF16),
            vm((6 * W, 3 * CH), BF16),
            vm((4 * W, LATENT), F32),
            vm((4 * W, LATENT), F32),
            vm((6 * W + 16, LATENT), F32),
            vm((4 * W, 3 * 256), BF16),
            vm((2 * W, CH), F32),
            vm((4 * W, 3 * LATENT), BF16),
            vm((2 * W, CH), F32),
            vm((8, 3 * JC, OWN), BF16),
            vm((NB, JC, CAP), BF16),
            vm((NB, 1, CAP), jnp.int32),
            vm((NB, 1, CAP), jnp.int32),
            vm((NB, LON, CAP), BF16),
            vm((NB, 2 * JC, CAP), F32),
            vm((NB, 1, CAP), F32),
            vm((NB, 1, CAP), F32),
            dma((2, 3)), dma((9,)), dma((9,)), dma((2, 9)), dma((2, 9)), dma, dma, dma((4, 2)), dma((4, 2)),
            dma((NB,)), dma((NB,)), dma((NB,)), dma((NB,)), dma, dma((NB,)), dma((NB,)),
        ],
        compiler_params=pltpu.CompilerParams(
            collective_id=0, has_side_effects=True, vmem_limit_bytes=60 * 1024 * 1024
        ),
    )(enc, dec, bias, x, seed, op, pos)


def local(
    analysed_fields,
    prediction_adjoint_seed,
    encoder_kernel_matrix,
    hidden_offset_term,
    decoder_kernel_matrix,
    measurement_wanted_positions,
    measurement_active_total,
    measurement_linear_operator,
):
    enc = jnp.transpose(encoder_kernel_matrix, (2, 3, 0, 1)).reshape(9, 64, FIELDS)
    dec = jnp.transpose(decoder_kernel_matrix, (2, 3, 1, 0)).reshape(9, 64, FIELDS)
    op = jnp.pad(jnp.transpose(measurement_linear_operator[0, 0], (1, 0, 2)), ((0, 0), (0, JC - FIELDS), (0, 0)))
    sensitivity, imp = fused(
        enc, dec, hidden_offset_term[None], analysed_fields, prediction_adjoint_seed, op,
        measurement_wanted_positions[0, 0])
    live = jnp.arange(CAP, dtype=jnp.int32)[None, :] < measurement_active_total[0, 0][:, None]
    impact = jnp.where(live, imp, jnp.float32(0.0))
    return (sensitivity, impact[None, None])


def solution(mesh):
    in_specs = (
        P(None, "band", None),
        P(None, "band", None),
        P("chan", None, None, None),
        P("chan"),
        P(None, "chan", None, None),
        P("band", "chan", None, None),
        P("band", "chan", None),
        P("band", "chan", None, None, None),
    )
    out_specs = (P(None, "band", "chan"), P("band", "chan", None, None))
    return jax.shard_map(local, mesh=mesh, in_specs=in_specs, out_specs=out_specs, check_vma=False)
```

```python
import jax
import jax.numpy as jnp
from jax import lax
from jax.experimental import pallas as pl
from jax.experimental.pallas import tpu as pltpu
from jax.sharding import PartitionSpec as P

MESH = pl.DeviceIdType.MESH
F32 = jnp.float32
BF16 = jnp.bfloat16

FIELDS = 227
CH = 256
NB = 16
NZ = 4
ROWS = 32
LON = 1024
OWN = 128
EDGE = 8
W = OWN + 2 * EDGE
JC = 240
CAP = 256
LATENT = 512
BESIDE_FIRST = 4
AWAY = (0, 4, 12, 8, 1, 15, 2, 14, 3, 13, 5, 11, 6, 10, 7, 9)
EARLY = 8


def dot(a, b):
    return lax.dot_general(a, b, (((1,), (0,)), ((), ())), preferred_element_type=F32)


def dot_nt(a, b):
    return lax.dot_general(a, b, (((1,), (1,)), ((), ())), preferred_element_type=F32)


def slope(u):
    s = jax.nn.sigmoid(u)
    return s * (1.0 + u * (1.0 - s))


def kernel(
    enc_ref, dec_ref, bias_ref, x_ref, seed_ref, op_ref, pos_ref, sens_ref, imp_ref,
    wts, raw, x, seed, xin, sdin, stin, midin, xb, sdb, pre1, lat2, sh, hb, s2, sb, mid,
    gt, low, opr, posb, posr, tent, part, impbuf, impin,
    rsem, wsend, wrecv, gsend, grecv, xsend, xrecv,
    psend, precv, osend, orecv, osem, isend, irecv,
):
    band = lax.axis_index("band")
    chan = lax.axis_index("chan")
    z = chan // 2
    core = chan % 2
    sib = (band, 2 * z + (1 - core))
    zp = (band, 2 * lax.rem(z + 1, NZ) + core)
    zm = (band, 2 * lax.rem(z + NZ - 1, NZ) + core)

    def at_band(d):
        return (lax.rem(band + (d + NB), NB), chan)

    fetches = []
    for n, ref in enumerate((x_ref, seed_ref)):
        for t in range(3):
            block = pl.ds(pl.multiple_of(lax.rem(chan + (t + 7), 8) * OWN, OWN), OWN)
            fetches.append(pltpu.make_async_copy(
                ref.at[:, :, block], raw.at[n, pl.ds(0, FIELDS), :, pl.ds(t * OWN, OWN)], rsem.at[n, t]))
    for c in fetches:
        c.start()

    barrier = pltpu.get_barrier_semaphore()
    across = [(lax.rem(band + NB + d, NB), 2 * lax.rem(z + dz, NZ) + core) for d in (-1, 0, 1) for dz in (1, 2, 3)]
    partners = [at_band(d) for d in range(1, NB)] + [sib] + across
    for dev in partners:
        pl.semaphore_signal(barrier, inc=1, device_id=dev, device_id_type=MESH)

    lrow = pl.multiple_of(core * 64, 64)
    for n, ref in enumerate((enc_ref, dec_ref)):
        for k in range(9):
            wts[9 * n + k, 0, pl.ds(lrow, 64), 0:128] = ref[k, :, 0:128]
            rest = jnp.concatenate([ref[k, :, 128:FIELDS], jnp.zeros((64, CH - FIELDS), BF16)], axis=1)
            if n == 0 and k == 4:
                eye = lax.broadcasted_iota(jnp.int32, (64, 64), 0) == lax.broadcasted_iota(jnp.int32, (64, 64), 1)
                bias = jnp.sum(jnp.where(eye, bias_ref[...], 0.0), axis=1, keepdims=True)
                high = bias.astype(BF16).astype(F32)
                middle = (bias - high).astype(BF16).astype(F32)
                least = bias - high - middle
                lane = lax.broadcasted_iota(jnp.int32, (64, 128), 1) + 128
                terms = jnp.where(lane == FIELDS, high, jnp.where(lane == FIELDS + 1, middle, least))
                terms = jnp.where(jnp.logical_and(lane >= FIELDS, lane < FIELDS + 3), terms, 0.0)
                rest = (rest.astype(F32) + terms).astype(BF16)
            wts[9 * n + k, 0, pl.ds(lrow, 64), 128:256] = rest

    pl.semaphore_wait(barrier, len(partners))

    def copy(src, dst, ss, rs, dev):
        return pltpu.make_async_remote_copy(
            src_ref=src, dst_ref=dst, send_sem=ss, recv_sem=rs, device_id=dev, device_id_type=MESH
        )

    def gather(region, half, ss, rs):
        return [
            copy(region(0), region(0), ss.at[0], rs.at[0], sib),
            copy(region(0), region(1), ss.at[1], rs.at[1], zp),
            copy(region(0), region(2), ss.at[2], rs.at[2], zm),
            copy(region(1), region(1), ss.at[3], rs.at[3], sib),
            copy(region(2), region(2), ss.at[4], rs.at[4], sib),
            copy(half(1, 0), half(3, 0), ss.at[5], rs.at[5], zp),
            copy(half(2, 1), half(3, 1), ss.at[6], rs.at[6], zm),
            copy(half(3, 0), half(3, 0), ss.at[7], rs.at[7], sib),
            copy(half(3, 1), half(3, 1), ss.at[8], rs.at[8], sib),
        ]

    wcopies = gather(
        lambda q: wts.at[:, q, pl.ds(lrow, 64), :],
        lambda q, h: wts.at[pl.ds(9 * h, 9), q, pl.ds(lrow, 64), :],
        wsend, wrecv,
    )
    for c in wcopies[:3]:
        c.start()

    def exchange(ref, n):
        own = ref.at[pl.ds(288, 288), :]
        return [
            copy(own, ref.at[pl.ds(0, 288), :], xsend.at[n, 0], xrecv.at[n, 0], at_band(1)),
            copy(own, ref.at[pl.ds(576, 288), :], xsend.at[n, 1], xrecv.at[n, 1], at_band(-1)),
        ]

    halos = [exchange(ref, n) for n, ref in enumerate((xin, sdin, stin, midin))]
    for n, (ref, own, fill) in enumerate(((x, xin, 1.0), (seed, sdin, 0.0))):
        for t in range(3):
            fetches[3 * n + t].wait()
        channel = lax.broadcasted_iota(jnp.int32, (CH - 224, 3 * OWN), 0) + 224
        for r in range(2):
            tail = raw[n, 224:CH, r, :]
            tail = jnp.where(channel < FIELDS, tail, jnp.where(channel < FIELDS + 3, fill, 0.0))
            rows = jnp.concatenate([raw[n, 0:224, r, :], tail], axis=0)
            ref[r * W:r * W + EDGE, :] = jnp.transpose(rows[:, 0:OWN])[OWN - EDGE:, :]
            ref[r * W + EDGE:r * W + EDGE + OWN, :] = jnp.transpose(rows[:, OWN:2 * OWN])
            ref[r * W + EDGE + OWN:(r + 1) * W, :] = jnp.transpose(rows[:, 2 * OWN:3 * OWN])[:EDGE, :]
        own[288:576, :] = ref[...].astype(BF16)
        for c in halos[n]:
            c.start()

    def pcopy(k):
        return copy(posb.at[lax.rem(band + AWAY[k], NB)], posr.at[k], psend.at[k], precv.at[k], at_band(AWAY[k]))

    def ocopy(k):
        return copy(op_ref.at[lax.rem(band + AWAY[k], NB)], opr.at[k], osend.at[k], orecv.at[k], at_band(AWAY[k]))

    for k in range(NB):
        posb[k] = pos_ref[k:k + 1, :]
    posr[0] = posb[band]
    for k in range(1, NB):
        pcopy(k).start()
    own_op = pltpu.make_async_copy(op_ref.at[band], opr.at[0], osem)
    own_op.start()
    for k in range(1, EARLY):
        ocopy(k).start()

    def shift3(dst, rows, width, first, flip):
        for r in range(rows):
            at = 2 * band + (first + r)
            live = jnp.logical_and(at >= 0, at < ROWS)
            for b in range(3):
                v = sh[8 + r * W + b - 1:8 + r * W + b - 1 + W, :width]
                lane = (2 - b if flip else b) * width
                dst[r * W:(r + 1) * W, lane:lane + width] = jnp.where(live, v, 0.0).astype(BF16)

    def spread(dst, ref, flip):
        sh[8:8 + 6 * W, :CH] = ref[...].astype(F32)
        shift3(dst, 6, CH, -2, flip)

    def rows_of(ref, n, width):
        return jnp.concatenate([ref[a * W:a * W + n, :width] for a in range(3)], axis=1)

    def taps(first, flip, lat, axis):
        parts = []
        for a in range(3):
            k = first + 3 * (2 - a if flip else a)
            if axis == 0:
                part_ = wts[k:k + 3, lat]
                parts.append(part_.reshape(part_.shape[0] * part_.shape[1] * part_.shape[2], CH))
            else:
                for b in range(3):
                    part_ = wts[k + b, lat]
                    parts.append(part_.reshape(part_.shape[0] * part_.shape[1], CH))
        return jnp.concatenate(parts, axis=axis)

    for d in range(1, NB):
        pcopy(d).wait_recv()

    def build(d, _):
        lon = (posr[d] & (4 * LON - 1)).astype(F32) * 0.25
        for q, dz in enumerate((0, NZ - 1, 1, 2)):
            at = lax.rem(z + dz, NZ) * 256
            west = (lax.broadcasted_iota(jnp.int32, (256, CAP), 0) + at).astype(F32)
            gap = jnp.abs(west - lon)
            gap = jnp.minimum(gap, LON - gap)
            tent[d, q * 256:(q + 1) * 256, :] = jnp.maximum(1.0 - gap, 0.0).astype(BF16)
        return 0

    lax.fori_loop(0, NB, build, 0)

    wcopies[1].wait_recv()
    wcopies[5].start()
    wcopies[3].start()
    wcopies[2].wait_recv()
    wcopies[6].start()
    wcopies[4].start()
    for c in halos[0]:
        c.wait_recv()
    spread(xb, xin, False)
    s2[...] = x[...]

    def first_half(q, nq, parts):
        width, off = nq * 128, q * 128
        lat = pl.ds(q, nq)
        if "state" in parts:
            p = dot_nt(rows_of(xb, 4 * W, 3 * CH), taps(0, False, lat, 1))
            pre1[:, off:off + width] = p
            sh[8:8 + 4 * W, :width] = p * jax.nn.sigmoid(p)
            shift3(hb, 4, width, -1, False)
            s2[...] += dot(rows_of(hb, 2 * W, 3 * width), taps(9, False, lat, 0))
        if "seed" in parts:
            lat2[:, off:off + width] = dot_nt(rows_of(sdb, 4 * W, 3 * CH), taps(9, True, lat, 1))

    for c in halos[1]:
        c.wait_recv()
    spread(sdb, sdin, True)
    wcopies[0].wait_recv()

    wcopies[3].wait_recv()
    wcopies[4].wait_recv()
    first_half(0, 3, ("state", "seed"))
    wcopies[5].wait_recv()
    wcopies[7].start()
    wcopies[6].wait_recv()
    wcopies[8].start()
    wcopies[7].wait_recv()
    wcopies[8].wait_recv()
    first_half(3, 1, ("state",))
    stin[288:576, :] = s2[...].astype(BF16)
    for c in halos[2]:
        c.start()
    first_half(3, 1, ("seed",))

    for c in halos[2]:
        c.wait_recv()
    spread(xb, stin, False)

    def second(t, _):
        off = pl.multiple_of(t * 256, 256)
        p = dot_nt(rows_of(xb, 4 * W, 3 * CH), taps(0, False, pl.ds(2 * t, 2), 1))
        sh[8:8 + 4 * W, pl.ds(off, 256)] = lat2[:, pl.ds(off, 256)] * slope(p)
        return 0

    lax.fori_loop(0, 2, second, 0)
    shift3(sb, 4, LATENT, -1, True)
    mid[...] = seed[...] + dot(rows_of(sb, 2 * W, 3 * LATENT), taps(0, True, pl.ds(0, 4), 0))
    midin[288:576, :] = mid[...].astype(BF16)
    for c in halos[3]:
        c.start()
    for c in halos[3]:
        c.wait_recv()
    for k in range(EARLY, NB):
        ocopy(k).start()

    spread(sdb, midin, True)

    def first(t, _):
        off = pl.multiple_of(t * 256, 256)
        v = dot_nt(rows_of(sdb, 4 * W, 3 * CH), taps(9, True, pl.ds(2 * t, 2), 1))
        sh[8:8 + 4 * W, pl.ds(off, 256)] = v * slope(pre1[:, pl.ds(off, 256)])
        return 0

    lax.fori_loop(0, 2, first, 0)
    shift3(sb, 4, LATENT, -1, True)
    mid[...] += dot(rows_of(sb, 2 * W, 3 * LATENT), taps(0, True, pl.ds(0, 4), 0))
    for r in range(2):
        g = jnp.transpose(mid[r * W + EDGE:r * W + EDGE + OWN, :])
        sens_ref[:, r, :] = g[:FIELDS]
        gt[core, r * JC:(r + 1) * JC, :] = g[:JC].astype(BF16)

    low[...] = jnp.where(band > 0, gt[core, 0:JC, :].astype(F32), 0.0).astype(BF16)
    own_rows, next_row = [], []
    for q, dz in enumerate((0, 1, NZ - 1, 2)):
        there = 2 * lax.rem(z + dz, NZ) + core
        if q > 0:
            own_rows.append(copy(
                gt.at[core, pl.ds(0, 2 * JC), :], gt.at[2 * q + core, pl.ds(0, 2 * JC), :],
                gsend.at[0, q], grecv.at[0, q], (band, there)))
        next_row.append(copy(
            low, gt.at[2 * q + core, pl.ds(2 * JC, JC), :], gsend.at[1, q], grecv.at[1, q],
            (lax.rem(band + NB - 1, NB), there)))
    own_shared = [copy(
        gt.at[2 * q + core, pl.ds(0, 2 * JC), :], gt.at[2 * q + core, pl.ds(0, 2 * JC), :],
        gsend.at[0, 4 + q], grecv.at[0, 4 + q], sib) for q in range(4)]
    next_shared = [copy(
        gt.at[2 * q + core, pl.ds(2 * JC, JC), :], gt.at[2 * q + core, pl.ds(2 * JC, JC), :],
        gsend.at[1, 4 + q], grecv.at[1, 4 + q], sib) for q in range(4)]
    for c in own_rows + next_row + own_shared[:1]:
        c.start()
    own_shared[0].wait_recv()

    def near(d, _):
        part[d] = dot(jnp.concatenate([gt[n, 0:2 * JC] for n in range(2)], axis=1), tent[d, 0:256])
        return 0

    lax.fori_loop(0, NB, near, 0)
    for q in range(1, 4):
        own_rows[q - 1].wait_recv()
        own_shared[q].start()
    for q in range(1, 4):
        own_shared[q].wait_recv()

    def beside(d, _):
        part[d] += dot(jnp.concatenate([gt[n, 0:2 * JC] for n in range(2, 8)], axis=1), tent[d, 256:1024])
        return 0

    lax.fori_loop(0, BESIDE_FIRST, beside, 0)
    for q in range(4):
        next_row[q].wait_recv()
        next_shared[q].start()
    lax.fori_loop(BESIDE_FIRST, NB, beside, 0)
    for q in range(4):
        next_shared[q].wait_recv()

    def icopy(k):
        return copy(impbuf.at[k], impin.at[band], isend.at[k], irecv.at[k], at_band(-AWAY[k]))

    def observe(d, _):
        m = part[d]
        m2 = dot(jnp.concatenate([gt[n, 2 * JC:3 * JC] for n in range(8)], axis=1), tent[d])
        row = (posr[d] // (4 * LON)).astype(F32) * 0.25
        col = jnp.maximum(1.0 - row, 0.0) * m[0:JC]
        col += jnp.maximum(1.0 - jnp.abs(row - 1.0), 0.0) * m[JC:2 * JC]
        col += jnp.maximum(row - 1.0, 0.0) * m2
        impbuf[d] = jnp.sum(col * opr[d].astype(F32), axis=0, keepdims=True)
        return 0

    own_op.wait()
    for lo, hi in ((0, EARLY), (EARLY, 12), (12, NB)):
        for k in range(max(lo, 1), hi):
            ocopy(k).wait_recv()
        lax.fori_loop(lo, hi, observe, 0)
        for k in range(max(lo, 1), hi):
            icopy(k).start()
    impin[band] = impbuf[0]
    for k in range(1, NB):
        copy(impbuf.at[k], impin.at[lax.rem(band + AWAY[k], NB)], isend.at[k], irecv.at[k], at_band(-AWAY[k])).wait_recv()
    for k in range(NB):
        imp_ref[k:k + 1, :] = impin[k]
    for c in wcopies + sum(halos, []) + own_rows + own_shared + next_row + next_shared:
        c.wait_send()
    for k in range(1, NB):
        pcopy(k).wait_send()
        ocopy(k).wait_send()
        icopy(k).wait_send()


def fused(enc, dec, bias, x, seed, op, pos):
    def vm(shape, dtype):
        return pltpu.VMEM(shape, dtype)

    vmem, anywhere = pl.BlockSpec(memory_space=pltpu.VMEM), pl.BlockSpec(memory_space=pl.ANY)
    dma = pltpu.SemaphoreType.DMA
    return pl.pallas_call(
        kernel,
        out_shape=(
            jax.ShapeDtypeStruct((FIELDS, 2, OWN), F32),
            jax.ShapeDtypeStruct((NB, CAP), F32),
        ),
        in_specs=[vmem, vmem, vmem, anywhere, anywhere, anywhere, vmem],
        out_specs=(vmem, vmem),
        scratch_shapes=[
            vm((18, 4, 128, CH), BF16),
            vm((2, CH, 2, 3 * OWN), F32),
            vm((2 * W, CH), F32),
            vm((2 * W, CH), F32),
            vm((6 * W, CH), BF16),
            vm((6 * W, CH), BF16),
            vm((6 * W, CH), BF16),
            vm((6 * W, CH), BF16),
            vm((6 * W, 3 * CH), BF16),
            vm((6 * W, 3 * CH), BF16),
            vm((4 * W, LATENT), F32),
            vm((4 * W, LATENT), F32),
            vm((6 * W + 16, LATENT), F32),
            vm((4 * W, 3 * 384), BF16),
            vm((2 * W, CH), F32),
            vm((4 * W, 3 * LATENT), BF16),
            vm((2 * W, CH), F32),
            vm((8, 3 * JC, OWN), BF16),
            vm((JC, OWN), BF16),
            vm((NB, JC, CAP), BF16),
            vm((NB, 1, CAP), jnp.int32),
            vm((NB, 1, CAP), jnp.int32),
            vm((NB, LON, CAP), BF16),
            vm((NB, 2 * JC, CAP), F32),
            vm((NB, 1, CAP), F32),
            vm((NB, 1, CAP), F32),
            dma((2, 3)), dma((9,)), dma((9,)), dma((2, 8)), dma((2, 8)), dma((4, 2)), dma((4, 2)),
            dma((NB,)), dma((NB,)), dma((NB,)), dma((NB,)), dma, dma((NB,)), dma((NB,)),
        ],
        compiler_params=pltpu.CompilerParams(
            collective_id=0, has_side_effects=True, vmem_limit_bytes=60 * 1024 * 1024
        ),
    )(enc, dec, bias, x, seed, op, pos)


def local(
    analysed_fields,
    prediction_adjoint_seed,
    encoder_kernel_matrix,
    hidden_offset_term,
    decoder_kernel_matrix,
    measurement_wanted_positions,
    measurement_active_total,
    measurement_linear_operator,
):
    enc = jnp.transpose(encoder_kernel_matrix, (2, 3, 0, 1)).reshape(9, 64, FIELDS)
    dec = jnp.transpose(decoder_kernel_matrix, (2, 3, 1, 0)).reshape(9, 64, FIELDS)
    op = jnp.pad(jnp.transpose(measurement_linear_operator[0, 0], (1, 0, 2)), ((0, 0), (0, JC - FIELDS), (0, 0)))
    sensitivity, imp = fused(
        enc, dec, hidden_offset_term[None], analysed_fields, prediction_adjoint_seed, op,
        measurement_wanted_positions[0, 0])
    live = jnp.arange(CAP, dtype=jnp.int32)[None, :] < measurement_active_total[0, 0][:, None]
    impact = jnp.where(live, imp, jnp.float32(0.0))
    return (sensitivity, impact[None, None])


def solution(mesh):
    in_specs = (
        P(None, "band", None),
        P(None, "band", None),
        P("chan", None, None, None),
        P("chan"),
        P(None, "chan", None, None),
        P("band", "chan", None, None),
        P("band", "chan", None),
        P("band", "chan", None, None, None),
    )
    out_specs = (P(None, "band", "chan"), P("band", "chan", None, None))
    return jax.shard_map(local, mesh=mesh, in_specs=in_specs, out_specs=out_specs, check_vma=False)
```

```python
import jax
import jax.numpy as jnp
from jax import lax
from jax.experimental import pallas as pl
from jax.experimental.pallas import tpu as pltpu
from jax.sharding import PartitionSpec as P

MESH = pl.DeviceIdType.MESH
F32 = jnp.float32
BF16 = jnp.bfloat16

FIELDS = 227
CH = 256
NB = 16
NZ = 4
ROWS = 32
LON = 1024
OWN = 128
EDGE = 8
W = OWN + 2 * EDGE
JC = 240
CAP = 256
LATENT = 512
AWAY = (0, 4, 12, 8, 1, 15, 2, 14, 3, 13, 5, 11, 6, 10, 7, 9)
EARLY = 12


def dot(a, b):
    return lax.dot_general(a, b, (((1,), (0,)), ((), ())), preferred_element_type=F32)


def dot_nt(a, b):
    return lax.dot_general(a, b, (((1,), (1,)), ((), ())), preferred_element_type=F32)


def slope(u):
    s = jax.nn.sigmoid(u)
    return s * (1.0 + u * (1.0 - s))


def kernel(
    enc_ref, dec_ref, bias_ref, x_ref, seed_ref, op_ref, pos_ref, sens_ref, imp_ref,
    wts, raw, x, seed, xin, sdin, stin, midin, xb, sdb, pre1, lat2, sh, hb, s2, sb, mid,
    gt, low, opw, opt, opr, posb, posr, tent, impbuf, impin,
    rsem, wsend, wrecv, gsend, grecv, xsend, xrecv,
    psend, precv, osend, orecv, osem, isend, irecv,
):
    band = lax.axis_index("band")
    chan = lax.axis_index("chan")
    z = chan // 2
    core = chan % 2
    sib = (band, 2 * z + (1 - core))
    zp = (band, 2 * lax.rem(z + 1, NZ) + core)
    zm = (band, 2 * lax.rem(z + NZ - 1, NZ) + core)

    def at_band(d):
        return (lax.rem(band + (d + NB), NB), chan)

    fetches = []
    for n, ref in enumerate((x_ref, seed_ref)):
        for t in range(3):
            block = pl.ds(pl.multiple_of(lax.rem(chan + (t + 7), 8) * OWN, OWN), OWN)
            fetches.append(pltpu.make_async_copy(
                ref.at[:, :, block], raw.at[n, pl.ds(0, FIELDS), :, pl.ds(t * OWN, OWN)], rsem.at[n, t]))
    op_fetch = pltpu.make_async_copy(op_ref, opw.at[pl.ds(0, FIELDS)], osem)
    for c in fetches + [op_fetch]:
        c.start()

    barrier = pltpu.get_barrier_semaphore()
    across = [(lax.rem(band + NB + d, NB), 2 * lax.rem(z + dz, NZ) + core) for d in (-1, 0, 1) for dz in (1, 2, 3)]
    partners = [at_band(d) for d in range(1, NB)] + [sib] + across
    for dev in partners:
        pl.semaphore_signal(barrier, inc=1, device_id=dev, device_id_type=MESH)

    lrow = pl.multiple_of(core * 64, 64)
    for n, ref in enumerate((enc_ref, dec_ref)):
        for k in range(9):
            wts[9 * n + k, 0, pl.ds(lrow, 64), 0:128] = ref[k, :, 0:128]
            rest = jnp.concatenate([ref[k, :, 128:FIELDS], jnp.zeros((64, CH - FIELDS), BF16)], axis=1)
            if n == 0 and k == 4:
                eye = lax.broadcasted_iota(jnp.int32, (64, 64), 0) == lax.broadcasted_iota(jnp.int32, (64, 64), 1)
                bias = jnp.sum(jnp.where(eye, bias_ref[...], 0.0), axis=1, keepdims=True)
                high = bias.astype(BF16).astype(F32)
                middle = (bias - high).astype(BF16).astype(F32)
                least = bias - high - middle
                lane = lax.broadcasted_iota(jnp.int32, (64, 128), 1) + 128
                terms = jnp.where(lane == FIELDS, high, jnp.where(lane == FIELDS + 1, middle, least))
                terms = jnp.where(jnp.logical_and(lane >= FIELDS, lane < FIELDS + 3), terms, 0.0)
                rest = (rest.astype(F32) + terms).astype(BF16)
            wts[9 * n + k, 0, pl.ds(lrow, 64), 128:256] = rest

    pl.semaphore_wait(barrier, len(partners))

    def copy(src, dst, ss, rs, dev):
        return pltpu.make_async_remote_copy(
            src_ref=src, dst_ref=dst, send_sem=ss, recv_sem=rs, device_id=dev, device_id_type=MESH
        )

    def gather(region, half, ss, rs):
        return [
            copy(region(0), region(0), ss.at[0], rs.at[0], sib),
            copy(region(0), region(1), ss.at[1], rs.at[1], zp),
            copy(region(0), region(2), ss.at[2], rs.at[2], zm),
            copy(region(1), region(1), ss.at[3], rs.at[3], sib),
            copy(region(2), region(2), ss.at[4], rs.at[4], sib),
            copy(half(1, 0), half(3, 0), ss.at[5], rs.at[5], zp),
            copy(half(2, 1), half(3, 1), ss.at[6], rs.at[6], zm),
            copy(half(3, 0), half(3, 0), ss.at[7], rs.at[7], sib),
            copy(half(3, 1), half(3, 1), ss.at[8], rs.at[8], sib),
        ]

    wcopies = gather(
        lambda q: wts.at[:, q, pl.ds(lrow, 64), :],
        lambda q, h: wts.at[pl.ds(9 * h, 9), q, pl.ds(lrow, 64), :],
        wsend, wrecv,
    )
    for c in wcopies[:3]:
        c.start()

    def exchange(ref, n):
        own = ref.at[pl.ds(288, 288), :]
        return [
            copy(own, ref.at[pl.ds(0, 288), :], xsend.at[n, 0], xrecv.at[n, 0], at_band(1)),
            copy(own, ref.at[pl.ds(576, 288), :], xsend.at[n, 1], xrecv.at[n, 1], at_band(-1)),
        ]

    halos = [exchange(ref, n) for n, ref in enumerate((xin, sdin, stin, midin))]
    for n, (ref, own, fill) in enumerate(((x, xin, 1.0), (seed, sdin, 0.0))):
        for t in range(3):
            fetches[3 * n + t].wait()
        channel = lax.broadcasted_iota(jnp.int32, (CH - 224, 3 * OWN), 0) + 224
        for r in range(2):
            tail = raw[n, 224:CH, r, :]
            tail = jnp.where(channel < FIELDS, tail, jnp.where(channel < FIELDS + 3, fill, 0.0))
            rows = jnp.concatenate([raw[n, 0:224, r, :], tail], axis=0)
            ref[r * W:r * W + EDGE, :] = jnp.transpose(rows[:, 0:OWN])[OWN - EDGE:, :]
            ref[r * W + EDGE:r * W + EDGE + OWN, :] = jnp.transpose(rows[:, OWN:2 * OWN])
            ref[r * W + EDGE + OWN:(r + 1) * W, :] = jnp.transpose(rows[:, 2 * OWN:3 * OWN])[:EDGE, :]
        own[288:576, :] = ref[...].astype(BF16)
        for c in halos[n]:
            c.start()

    def pcopy(k):
        return copy(posb.at[lax.rem(band + AWAY[k], NB)], posr.at[k], psend.at[k], precv.at[k], at_band(AWAY[k]))

    def ocopy(k):
        return copy(opt.at[lax.rem(band + AWAY[k], NB)], opr.at[k], osend.at[k], orecv.at[k], at_band(AWAY[k]))

    for k in range(NB):
        posb[k] = pos_ref[k:k + 1, :]
    posr[0] = posb[band]
    for k in range(1, NB):
        pcopy(k).start()
    op_fetch.wait()
    opw[FIELDS:JC] = jnp.zeros((JC - FIELDS, NB, CAP), BF16)

    def by_band(t, _):
        at = pl.ds(pl.multiple_of(16 * t, 16), 16)
        opt[:, at, :] = jnp.transpose(opw[at].astype(F32), (1, 0, 2)).astype(BF16)
        return 0

    lax.fori_loop(0, JC // 16, by_band, 0)

    def shift3(dst, rows, width, first, flip):
        for r in range(rows):
            at = 2 * band + (first + r)
            live = jnp.logical_and(at >= 0, at < ROWS)
            for b in range(3):
                v = sh[8 + r * W + b - 1:8 + r * W + b - 1 + W, :width]
                lane = (2 - b if flip else b) * width
                dst[r * W:(r + 1) * W, lane:lane + width] = jnp.where(live, v, 0.0).astype(BF16)

    def spread(dst, ref, flip):
        sh[8:8 + 6 * W, :CH] = ref[...].astype(F32)
        shift3(dst, 6, CH, -2, flip)

    def rows_of(ref, n, width):
        return jnp.concatenate([ref[a * W:a * W + n, :width] for a in range(3)], axis=1)

    def taps(first, flip, lat, axis):
        parts = []
        for a in range(3):
            k = first + 3 * (2 - a if flip else a)
            if axis == 0:
                part_ = wts[k:k + 3, lat]
                parts.append(part_.reshape(part_.shape[0] * part_.shape[1] * part_.shape[2], CH))
            else:
                for b in range(3):
                    part_ = wts[k + b, lat]
                    parts.append(part_.reshape(part_.shape[0] * part_.shape[1], CH))
        return jnp.concatenate(parts, axis=axis)

    for d in range(1, NB):
        pcopy(d).wait_recv()

    def build(d, _):
        lon = (posr[d] & (4 * LON - 1)).astype(F32) * 0.25
        for q, dz in enumerate((0, NZ - 1, 1, 2)):
            at = lax.rem(z + dz, NZ) * 256
            west = (lax.broadcasted_iota(jnp.int32, (256, CAP), 0) + at).astype(F32)
            gap = jnp.abs(west - lon)
            gap = jnp.minimum(gap, LON - gap)
            tent[d, q * 256:(q + 1) * 256, :] = jnp.maximum(1.0 - gap, 0.0).astype(BF16)
        return 0

    lax.fori_loop(0, NB, build, 0)

    for k in range(1, EARLY):
        ocopy(k).start()
    wcopies[1].wait_recv()
    wcopies[5].start()
    wcopies[3].start()
    wcopies[2].wait_recv()
    wcopies[6].start()
    wcopies[4].start()
    for c in halos[0]:
        c.wait_recv()
    spread(xb, xin, False)
    s2[...] = x[...]

    def first_half(q, nq, parts):
        width, off = nq * 128, q * 128
        lat = pl.ds(q, nq)
        if "state" in parts:
            p = dot_nt(rows_of(xb, 4 * W, 3 * CH), taps(0, False, lat, 1))
            pre1[:, off:off + width] = p
            sh[8:8 + 4 * W, :width] = p * jax.nn.sigmoid(p)
            shift3(hb, 4, width, -1, False)
            s2[...] += dot(rows_of(hb, 2 * W, 3 * width), taps(9, False, lat, 0))
        if "seed" in parts:
            lat2[:, off:off + width] = dot_nt(rows_of(sdb, 4 * W, 3 * CH), taps(9, True, lat, 1))

    for c in halos[1]:
        c.wait_recv()
    spread(sdb, sdin, True)
    wcopies[0].wait_recv()

    wcopies[3].wait_recv()
    wcopies[4].wait_recv()
    first_half(0, 3, ("state", "seed"))
    wcopies[5].wait_recv()
    wcopies[7].start()
    wcopies[6].wait_recv()
    wcopies[8].start()
    wcopies[7].wait_recv()
    wcopies[8].wait_recv()
    first_half(3, 1, ("state",))
    stin[288:576, :] = s2[...].astype(BF16)
    for c in halos[2]:
        c.start()
    first_half(3, 1, ("seed",))

    for c in halos[2]:
        c.wait_recv()
    spread(xb, stin, False)

    def second(t, _):
        off = pl.multiple_of(t * 256, 256)
        p = dot_nt(rows_of(xb, 4 * W, 3 * CH), taps(0, False, pl.ds(2 * t, 2), 1))
        sh[8:8 + 4 * W, pl.ds(off, 256)] = lat2[:, pl.ds(off, 256)] * slope(p)
        return 0

    lax.fori_loop(0, 2, second, 0)
    shift3(sb, 4, LATENT, -1, True)
    mid[...] = seed[...] + dot(rows_of(sb, 2 * W, 3 * LATENT), taps(0, True, pl.ds(0, 4), 0))
    midin[288:576, :] = mid[...].astype(BF16)
    for c in halos[3]:
        c.start()
    for c in halos[3]:
        c.wait_recv()
    for k in range(EARLY, NB):
        ocopy(k).start()

    spread(sdb, midin, True)

    def first(t, _):
        off = pl.multiple_of(t * 256, 256)
        v = dot_nt(rows_of(sdb, 4 * W, 3 * CH), taps(9, True, pl.ds(2 * t, 2), 1))
        sh[8:8 + 4 * W, pl.ds(off, 256)] = v * slope(pre1[:, pl.ds(off, 256)])
        return 0

    lax.fori_loop(0, 2, first, 0)
    shift3(sb, 4, LATENT, -1, True)
    mid[...] += dot(rows_of(sb, 2 * W, 3 * LATENT), taps(0, True, pl.ds(0, 4), 0))
    for r in range(2):
        g = jnp.transpose(mid[r * W + EDGE:r * W + EDGE + OWN, :])
        sens_ref[:, r, :] = g[:FIELDS]
        gt[core, r * JC:(r + 1) * JC, :] = g[:JC].astype(BF16)

    low[...] = jnp.where(band > 0, gt[core, 0:JC, :].astype(F32), 0.0).astype(BF16)
    own_rows, next_row = [], []
    for q, dz in enumerate((0, 1, NZ - 1, 2)):
        there = 2 * lax.rem(z + dz, NZ) + core
        if q > 0:
            own_rows.append(copy(
                gt.at[core, pl.ds(0, 2 * JC), :], gt.at[2 * q + core, pl.ds(0, 2 * JC), :],
                gsend.at[0, q], grecv.at[0, q], (band, there)))
        next_row.append(copy(
            low, gt.at[2 * q + core, pl.ds(2 * JC, JC), :], gsend.at[1, q], grecv.at[1, q],
            (lax.rem(band + NB - 1, NB), there)))
    own_shared = [copy(
        gt.at[2 * q + core, pl.ds(0, 2 * JC), :], gt.at[2 * q + core, pl.ds(0, 2 * JC), :],
        gsend.at[0, 4 + q], grecv.at[0, 4 + q], sib) for q in range(4)]
    next_shared = [copy(
        gt.at[2 * q + core, pl.ds(2 * JC, JC), :], gt.at[2 * q + core, pl.ds(2 * JC, JC), :],
        gsend.at[1, 4 + q], grecv.at[1, 4 + q], sib) for q in range(4)]
    for c in own_rows + next_row + own_shared[:1]:
        c.start()
    next_row[0].wait_recv()
    next_shared[0].start()
    own_shared[0].wait_recv()
    next_shared[0].wait_recv()

    for q in range(1, 4):
        own_rows[q - 1].wait_recv()
        own_shared[q].start()
    for q in range(1, 4):
        next_row[q].wait_recv()
        next_shared[q].start()
    for q in range(1, 4):
        own_shared[q].wait_recv()
        next_shared[q].wait_recv()

    def icopy(k):
        return copy(impbuf.at[k], impin.at[band], isend.at[k], irecv.at[k], at_band(-AWAY[k]))

    def observe(d, _):
        m = dot(jnp.concatenate([gt[n] for n in range(8)], axis=1), tent[d])
        row = (posr[d] // (4 * LON)).astype(F32) * 0.25
        col = jnp.maximum(1.0 - row, 0.0) * m[0:JC]
        col += jnp.maximum(1.0 - jnp.abs(row - 1.0), 0.0) * m[JC:2 * JC]
        col += jnp.maximum(row - 1.0, 0.0) * m[2 * JC:3 * JC]
        impbuf[d] = jnp.sum(col * opr[d].astype(F32), axis=0, keepdims=True)
        return 0

    opr[0] = opt[band]
    for lo, hi in ((0, EARLY), (EARLY, 12), (12, NB)):
        for k in range(max(lo, 1), hi):
            ocopy(k).wait_recv()
        lax.fori_loop(lo, hi, observe, 0)
        for k in range(max(lo, 1), hi):
            icopy(k).start()
    impin[band] = impbuf[0]
    for k in range(1, NB):
        copy(impbuf.at[k], impin.at[lax.rem(band + AWAY[k], NB)], isend.at[k], irecv.at[k], at_band(-AWAY[k])).wait_recv()
    for k in range(NB):
        imp_ref[k:k + 1, :] = impin[k]
    for c in wcopies + sum(halos, []) + own_rows + own_shared + next_row + next_shared:
        c.wait_send()
    for k in range(1, NB):
        pcopy(k).wait_send()
        ocopy(k).wait_send()
        icopy(k).wait_send()


def fused(enc, dec, bias, x, seed, op, pos):
    def vm(shape, dtype):
        return pltpu.VMEM(shape, dtype)

    vmem, anywhere = pl.BlockSpec(memory_space=pltpu.VMEM), pl.BlockSpec(memory_space=pl.ANY)
    dma = pltpu.SemaphoreType.DMA
    return pl.pallas_call(
        kernel,
        out_shape=(
            jax.ShapeDtypeStruct((FIELDS, 2, OWN), F32),
            jax.ShapeDtypeStruct((NB, CAP), F32),
        ),
        in_specs=[vmem, vmem, vmem, anywhere, anywhere, anywhere, vmem],
        out_specs=(vmem, vmem),
        scratch_shapes=[
            vm((18, 4, 128, CH), BF16),
            vm((2, CH, 2, 3 * OWN), F32),
            vm((2 * W, CH), F32),
            vm((2 * W, CH), F32),
            vm((6 * W, CH), BF16),
            vm((6 * W, CH), BF16),
            vm((6 * W, CH), BF16),
            vm((6 * W, CH), BF16),
            vm((6 * W, 3 * CH), BF16),
            vm((6 * W, 3 * CH), BF16),
            vm((4 * W, LATENT), F32),
            vm((4 * W, LATENT), F32),
            vm((6 * W + 16, LATENT), F32),
            vm((4 * W, 3 * 384), BF16),
            vm((2 * W, CH), F32),
            vm((4 * W, 3 * LATENT), BF16),
            vm((2 * W, CH), F32),
            vm((8, 3 * JC, OWN), BF16),
            vm((JC, OWN), BF16),
            vm((JC, NB, CAP), BF16),
            vm((NB, JC, CAP), BF16),
            vm((NB, JC, CAP), BF16),
            vm((NB, 1, CAP), jnp.int32),
            vm((NB, 1, CAP), jnp.int32),
            vm((NB, LON, CAP), BF16),
            vm((NB, 1, CAP), F32),
            vm((NB, 1, CAP), F32),
            dma((2, 3)), dma((9,)), dma((9,)), dma((2, 8)), dma((2, 8)), dma((4, 2)), dma((4, 2)),
            dma((NB,)), dma((NB,)), dma((NB,)), dma((NB,)), dma, dma((NB,)), dma((NB,)),
        ],
        compiler_params=pltpu.CompilerParams(
            collective_id=0, has_side_effects=True, vmem_limit_bytes=60 * 1024 * 1024
        ),
    )(enc, dec, bias, x, seed, op, pos)


def local(
    analysed_fields,
    prediction_adjoint_seed,
    encoder_kernel_matrix,
    hidden_offset_term,
    decoder_kernel_matrix,
    measurement_wanted_positions,
    measurement_active_total,
    measurement_linear_operator,
):
    enc = jnp.transpose(encoder_kernel_matrix, (2, 3, 0, 1)).reshape(9, 64, FIELDS)
    dec = jnp.transpose(decoder_kernel_matrix, (2, 3, 1, 0)).reshape(9, 64, FIELDS)
    op = measurement_linear_operator[0, 0]
    sensitivity, imp = fused(
        enc, dec, hidden_offset_term[None], analysed_fields, prediction_adjoint_seed, op,
        measurement_wanted_positions[0, 0])
    live = jnp.arange(CAP, dtype=jnp.int32)[None, :] < measurement_active_total[0, 0][:, None]
    impact = jnp.where(live, imp, jnp.float32(0.0))
    return (sensitivity, impact[None, None])


def solution(mesh):
    in_specs = (
        P(None, "band", None),
        P(None, "band", None),
        P("chan", None, None, None),
        P("chan"),
        P(None, "chan", None, None),
        P("band", "chan", None, None),
        P("band", "chan", None),
        P("band", "chan", None, None, None),
    )
    out_specs = (P(None, "band", "chan"), P("band", "chan", None, None))
    return jax.shard_map(local, mesh=mesh, in_specs=in_specs, out_specs=out_specs, check_vma=False)
```

```python
import jax
import jax.numpy as jnp
from jax import lax
from jax.experimental import pallas as pl
from jax.experimental.pallas import tpu as pltpu
from jax.sharding import PartitionSpec as P

MESH = pl.DeviceIdType.MESH
F32 = jnp.float32
BF16 = jnp.bfloat16

FIELDS = 227
CH = 256
NB = 16
NZ = 4
ROWS = 32
LON = 1024
OWN = 128
EDGE = 8
W = OWN + 2 * EDGE
JC = 240
CAP = 256
LATENT = 512
AWAY = (0, 4, 12, 8, 1, 15, 2, 14, 3, 13, 5, 11, 6, 10, 7, 9)
EARLY = 12


def dot(a, b):
    return lax.dot_general(a, b, (((1,), (0,)), ((), ())), preferred_element_type=F32)


def dot_nt(a, b):
    return lax.dot_general(a, b, (((1,), (1,)), ((), ())), preferred_element_type=F32)


def slope(u):
    s = jax.nn.sigmoid(u)
    return s * (1.0 + u * (1.0 - s))


def kernel(
    enc_ref, dec_ref, bias_ref, x_ref, seed_ref, op_ref, pos_ref, live_ref, sens_ref, imp_ref,
    wts, raw, x, seed, xin, sdin, stin, midin, xb, sdb, pre1, lat2, sh, hb, s2, sb, mid,
    gt, low, opw, opt, opr, posb, posr, tent, impbuf, impin,
    rsem, wsend, wrecv, gsend, grecv, xsend, xrecv,
    psend, precv, osend, orecv, osem, isend, irecv,
):
    band = lax.axis_index("band")
    chan = lax.axis_index("chan")
    z = chan // 2
    core = chan % 2
    sib = (band, 2 * z + (1 - core))
    zp = (band, 2 * lax.rem(z + 1, NZ) + core)
    zm = (band, 2 * lax.rem(z + NZ - 1, NZ) + core)

    def at_band(d):
        return (lax.rem(band + (d + NB), NB), chan)

    fetches = []
    for n, ref in enumerate((x_ref, seed_ref)):
        for t in range(3):
            block = pl.ds(pl.multiple_of(lax.rem(chan + (t + 7), 8) * OWN, OWN), OWN)
            fetches.append(pltpu.make_async_copy(
                ref.at[:, :, block], raw.at[n, pl.ds(0, FIELDS), :, pl.ds(t * OWN, OWN)], rsem.at[n, t]))
    op_fetch = pltpu.make_async_copy(op_ref, opw.at[pl.ds(0, FIELDS)], osem)
    for c in fetches + [op_fetch]:
        c.start()

    barrier = pltpu.get_barrier_semaphore()
    across = [(lax.rem(band + NB + d, NB), 2 * lax.rem(z + dz, NZ) + core) for d in (-1, 0, 1) for dz in (1, 2, 3)]
    partners = [at_band(d) for d in range(1, NB)] + [sib] + across
    for dev in partners:
        pl.semaphore_signal(barrier, inc=1, device_id=dev, device_id_type=MESH)

    lrow = pl.multiple_of(core * 64, 64)
    for n, ref in enumerate((enc_ref, dec_ref)):
        for k in range(9):
            wts[9 * n + k, 0, pl.ds(lrow, 64), 0:128] = ref[k, :, 0:128]
            rest = jnp.concatenate([ref[k, :, 128:FIELDS], jnp.zeros((64, CH - FIELDS), BF16)], axis=1)
            if n == 0 and k == 4:
                eye = lax.broadcasted_iota(jnp.int32, (64, 64), 0) == lax.broadcasted_iota(jnp.int32, (64, 64), 1)
                bias = jnp.sum(jnp.where(eye, bias_ref[...], 0.0), axis=1, keepdims=True)
                high = bias.astype(BF16).astype(F32)
                middle = (bias - high).astype(BF16).astype(F32)
                least = bias - high - middle
                lane = lax.broadcasted_iota(jnp.int32, (64, 128), 1) + 128
                terms = jnp.where(lane == FIELDS, high, jnp.where(lane == FIELDS + 1, middle, least))
                terms = jnp.where(jnp.logical_and(lane >= FIELDS, lane < FIELDS + 3), terms, 0.0)
                rest = (rest.astype(F32) + terms).astype(BF16)
            wts[9 * n + k, 0, pl.ds(lrow, 64), 128:256] = rest

    pl.semaphore_wait(barrier, len(partners))

    def copy(src, dst, ss, rs, dev):
        return pltpu.make_async_remote_copy(
            src_ref=src, dst_ref=dst, send_sem=ss, recv_sem=rs, device_id=dev, device_id_type=MESH
        )

    def gather(region, half, ss, rs):
        return [
            copy(region(0), region(0), ss.at[0], rs.at[0], sib),
            copy(region(0), region(1), ss.at[1], rs.at[1], zp),
            copy(region(0), region(2), ss.at[2], rs.at[2], zm),
            copy(region(1), region(1), ss.at[3], rs.at[3], sib),
            copy(region(2), region(2), ss.at[4], rs.at[4], sib),
            copy(half(1, 0), half(3, 0), ss.at[5], rs.at[5], zp),
            copy(half(2, 1), half(3, 1), ss.at[6], rs.at[6], zm),
            copy(half(3, 0), half(3, 0), ss.at[7], rs.at[7], sib),
            copy(half(3, 1), half(3, 1), ss.at[8], rs.at[8], sib),
        ]

    wcopies = gather(
        lambda q: wts.at[:, q, pl.ds(lrow, 64), :],
        lambda q, h: wts.at[pl.ds(9 * h, 9), q, pl.ds(lrow, 64), :],
        wsend, wrecv,
    )
    for c in wcopies[:3]:
        c.start()

    def exchange(ref, n):
        own = ref.at[pl.ds(288, 288), :]
        return [
            copy(own, ref.at[pl.ds(0, 288), :], xsend.at[n, 0], xrecv.at[n, 0], at_band(1)),
            copy(own, ref.at[pl.ds(576, 288), :], xsend.at[n, 1], xrecv.at[n, 1], at_band(-1)),
        ]

    halos = [exchange(ref, n) for n, ref in enumerate((xin, sdin, stin, midin))]
    for n, (ref, own, fill) in enumerate(((x, xin, 1.0), (seed, sdin, 0.0))):
        for t in range(3):
            fetches[3 * n + t].wait()
        channel = lax.broadcasted_iota(jnp.int32, (CH - 224, 3 * OWN), 0) + 224
        for r in range(2):
            tail = raw[n, 224:CH, r, :]
            tail = jnp.where(channel < FIELDS, tail, jnp.where(channel < FIELDS + 3, fill, 0.0))
            rows = jnp.concatenate([raw[n, 0:224, r, :], tail], axis=0)
            ref[r * W:r * W + EDGE, :] = jnp.transpose(rows[:, 0:OWN])[OWN - EDGE:, :]
            ref[r * W + EDGE:r * W + EDGE + OWN, :] = jnp.transpose(rows[:, OWN:2 * OWN])
            ref[r * W + EDGE + OWN:(r + 1) * W, :] = jnp.transpose(rows[:, 2 * OWN:3 * OWN])[:EDGE, :]
        own[288:576, :] = ref[...].astype(BF16)
        for c in halos[n]:
            c.start()

    def pcopy(k):
        return copy(posb.at[lax.rem(band + AWAY[k], NB)], posr.at[k], psend.at[k], precv.at[k], at_band(AWAY[k]))

    def ocopy(k):
        return copy(opt.at[lax.rem(band + AWAY[k], NB)], opr.at[k], osend.at[k], orecv.at[k], at_band(AWAY[k]))

    for k in range(NB):
        posb[k] = pos_ref[k:k + 1, :]
    posr[0] = posb[band]
    for k in range(1, NB):
        pcopy(k).start()
    op_fetch.wait()
    opw[FIELDS:JC] = jnp.zeros((JC - FIELDS, NB, CAP), BF16)

    def by_band(t, _):
        at = pl.ds(pl.multiple_of(16 * t, 16), 16)
        opt[:, at, :] = jnp.transpose(opw[at].astype(F32), (1, 0, 2)).astype(BF16)
        return 0

    lax.fori_loop(0, JC // 16, by_band, 0)

    def shift3(dst, rows, width, first, flip):
        for r in range(rows):
            at = 2 * band + (first + r)
            live = jnp.logical_and(at >= 0, at < ROWS)
            for b in range(3):
                v = sh[8 + r * W + b - 1:8 + r * W + b - 1 + W, :width]
                lane = (2 - b if flip else b) * width
                dst[r * W:(r + 1) * W, lane:lane + width] = jnp.where(live, v, 0.0).astype(BF16)

    def spread(dst, ref, flip):
        sh[8:8 + 6 * W, :CH] = ref[...].astype(F32)
        shift3(dst, 6, CH, -2, flip)

    def rows_of(ref, n, width):
        return jnp.concatenate([ref[a * W:a * W + n, :width] for a in range(3)], axis=1)

    def taps(first, flip, lat, axis):
        parts = []
        for a in range(3):
            k = first + 3 * (2 - a if flip else a)
            if axis == 0:
                part_ = wts[k:k + 3, lat]
                parts.append(part_.reshape(part_.shape[0] * part_.shape[1] * part_.shape[2], CH))
            else:
                for b in range(3):
                    part_ = wts[k + b, lat]
                    parts.append(part_.reshape(part_.shape[0] * part_.shape[1], CH))
        return jnp.concatenate(parts, axis=axis)

    for d in range(1, NB):
        pcopy(d).wait_recv()

    def build(d, _):
        lon = (posr[d] & (4 * LON - 1)).astype(F32) * 0.25
        for q, dz in enumerate((0, NZ - 1, 1, 2)):
            at = lax.rem(z + dz, NZ) * 256
            west = (lax.broadcasted_iota(jnp.int32, (256, CAP), 0) + at).astype(F32)
            gap = jnp.abs(west - lon)
            gap = jnp.minimum(gap, LON - gap)
            tent[d, q * 256:(q + 1) * 256, :] = jnp.maximum(1.0 - gap, 0.0).astype(BF16)
        return 0

    lax.fori_loop(0, NB, build, 0)

    for k in range(1, EARLY):
        ocopy(k).start()
    wcopies[1].wait_recv()
    wcopies[5].start()
    wcopies[3].start()
    wcopies[2].wait_recv()
    wcopies[6].start()
    wcopies[4].start()
    for c in halos[0]:
        c.wait_recv()
    spread(xb, xin, False)
    s2[...] = x[...]

    def first_half(q, nq, parts):
        width, off = nq * 128, q * 128
        lat = pl.ds(q, nq)
        if "state" in parts:
            p = dot_nt(rows_of(xb, 4 * W, 3 * CH), taps(0, False, lat, 1))
            pre1[:, off:off + width] = p
            sh[8:8 + 4 * W, :width] = p * jax.nn.sigmoid(p)
            shift3(hb, 4, width, -1, False)
            s2[...] += dot(rows_of(hb, 2 * W, 3 * width), taps(9, False, lat, 0))
        if "seed" in parts:
            lat2[:, off:off + width] = dot_nt(rows_of(sdb, 4 * W, 3 * CH), taps(9, True, lat, 1))

    for c in halos[1]:
        c.wait_recv()
    spread(sdb, sdin, True)
    wcopies[0].wait_recv()

    wcopies[3].wait_recv()
    wcopies[4].wait_recv()
    first_half(0, 3, ("state", "seed"))
    wcopies[5].wait_recv()
    wcopies[7].start()
    wcopies[6].wait_recv()
    wcopies[8].start()
    wcopies[7].wait_recv()
    wcopies[8].wait_recv()
    first_half(3, 1, ("state",))
    stin[288:576, :] = s2[...].astype(BF16)
    for c in halos[2]:
        c.start()
    first_half(3, 1, ("seed",))

    for c in halos[2]:
        c.wait_recv()
    spread(xb, stin, False)

    def second(t, _):
        off = pl.multiple_of(t * 256, 256)
        p = dot_nt(rows_of(xb, 4 * W, 3 * CH), taps(0, False, pl.ds(2 * t, 2), 1))
        sh[8:8 + 4 * W, pl.ds(off, 256)] = lat2[:, pl.ds(off, 256)] * slope(p)
        return 0

    lax.fori_loop(0, 2, second, 0)
    shift3(sb, 4, LATENT, -1, True)
    mid[...] = seed[...] + dot(rows_of(sb, 2 * W, 3 * LATENT), taps(0, True, pl.ds(0, 4), 0))
    midin[288:576, :] = mid[...].astype(BF16)
    for c in halos[3]:
        c.start()
    for c in halos[3]:
        c.wait_recv()
    for k in range(EARLY, NB):
        ocopy(k).start()

    spread(sdb, midin, True)

    def first(t, _):
        off = pl.multiple_of(t * 256, 256)
        v = dot_nt(rows_of(sdb, 4 * W, 3 * CH), taps(9, True, pl.ds(2 * t, 2), 1))
        sh[8:8 + 4 * W, pl.ds(off, 256)] = v * slope(pre1[:, pl.ds(off, 256)])
        return 0

    lax.fori_loop(0, 2, first, 0)
    shift3(sb, 4, LATENT, -1, True)
    mid[...] += dot(rows_of(sb, 2 * W, 3 * LATENT), taps(0, True, pl.ds(0, 4), 0))
    for r in range(2):
        g = jnp.transpose(mid[r * W + EDGE:r * W + EDGE + OWN, :])
        sens_ref[:, r, :] = g[:FIELDS]
        gt[core, r * JC:(r + 1) * JC, :] = g[:JC].astype(BF16)

    low[...] = jnp.where(band > 0, gt[core, 0:JC, :].astype(F32), 0.0).astype(BF16)
    own_rows, next_row = [], []
    for q, dz in enumerate((0, 1, NZ - 1, 2)):
        there = 2 * lax.rem(z + dz, NZ) + core
        if q > 0:
            own_rows.append(copy(
                gt.at[core, pl.ds(0, 2 * JC), :], gt.at[2 * q + core, pl.ds(0, 2 * JC), :],
                gsend.at[0, q], grecv.at[0, q], (band, there)))
        next_row.append(copy(
            low, gt.at[2 * q + core, pl.ds(2 * JC, JC), :], gsend.at[1, q], grecv.at[1, q],
            (lax.rem(band + NB - 1, NB), there)))
    own_shared = [copy(
        gt.at[2 * q + core, pl.ds(0, 2 * JC), :], gt.at[2 * q + core, pl.ds(0, 2 * JC), :],
        gsend.at[0, 4 + q], grecv.at[0, 4 + q], sib) for q in range(4)]
    next_shared = [copy(
        gt.at[2 * q + core, pl.ds(2 * JC, JC), :], gt.at[2 * q + core, pl.ds(2 * JC, JC), :],
        gsend.at[1, 4 + q], grecv.at[1, 4 + q], sib) for q in range(4)]
    for c in own_rows + next_row + own_shared[:1]:
        c.start()
    next_row[0].wait_recv()
    next_shared[0].start()
    own_shared[0].wait_recv()
    next_shared[0].wait_recv()

    for q in range(1, 4):
        own_rows[q - 1].wait_recv()
        own_shared[q].start()
    for q in range(1, 4):
        next_row[q].wait_recv()
        next_shared[q].start()
    for q in range(1, 4):
        own_shared[q].wait_recv()
        next_shared[q].wait_recv()

    def icopy(k):
        return copy(impbuf.at[k], impin.at[band], isend.at[k], irecv.at[k], at_band(-AWAY[k]))

    def observe(d, _):
        m = dot(jnp.concatenate([gt[n] for n in range(8)], axis=1), tent[d])
        row = (posr[d] // (4 * LON)).astype(F32) * 0.25
        col = jnp.maximum(1.0 - row, 0.0) * m[0:JC]
        col += jnp.maximum(1.0 - jnp.abs(row - 1.0), 0.0) * m[JC:2 * JC]
        col += jnp.maximum(row - 1.0, 0.0) * m[2 * JC:3 * JC]
        impbuf[d] = jnp.sum(col * opr[d].astype(F32), axis=0, keepdims=True)
        return 0

    opr[0] = opt[band]
    for lo, hi in ((0, EARLY), (EARLY, 12), (12, NB)):
        for k in range(max(lo, 1), hi):
            ocopy(k).wait_recv()
        lax.fori_loop(lo, hi, observe, 0)
        for k in range(max(lo, 1), hi):
            icopy(k).start()
    impin[band] = impbuf[0]
    for k in range(1, NB):
        copy(impbuf.at[k], impin.at[lax.rem(band + AWAY[k], NB)], isend.at[k], irecv.at[k], at_band(-AWAY[k])).wait_recv()
    diagonal = lax.broadcasted_iota(jnp.int32, (NB, NB), 0) == lax.broadcasted_iota(jnp.int32, (NB, NB), 1)
    total = jnp.sum(jnp.where(diagonal, live_ref[...].astype(F32), 0.0), axis=1, keepdims=True)
    answers = jnp.concatenate([impin[k] for k in range(NB)], axis=0)
    slots = lax.broadcasted_iota(jnp.int32, (NB, CAP), 1).astype(F32)
    imp_ref[...] = jnp.where(slots < total, answers, 0.0)
    for c in wcopies + sum(halos, []) + own_rows + own_shared + next_row + next_shared:
        c.wait_send()
    for k in range(1, NB):
        pcopy(k).wait_send()
        ocopy(k).wait_send()
        icopy(k).wait_send()


def fused(enc, dec, bias, x, seed, op, pos, live):
    def vm(shape, dtype):
        return pltpu.VMEM(shape, dtype)

    vmem, anywhere = pl.BlockSpec(memory_space=pltpu.VMEM), pl.BlockSpec(memory_space=pl.ANY)
    dma = pltpu.SemaphoreType.DMA
    return pl.pallas_call(
        kernel,
        out_shape=(
            jax.ShapeDtypeStruct((FIELDS, 2, OWN), F32),
            jax.ShapeDtypeStruct((NB, CAP), F32),
        ),
        in_specs=[vmem, vmem, vmem, anywhere, anywhere, anywhere, vmem, vmem],
        out_specs=(vmem, vmem),
        scratch_shapes=[
            vm((18, 4, 128, CH), BF16),
            vm((2, CH, 2, 3 * OWN), F32),
            vm((2 * W, CH), F32),
            vm((2 * W, CH), F32),
            vm((6 * W, CH), BF16),
            vm((6 * W, CH), BF16),
            vm((6 * W, CH), BF16),
            vm((6 * W, CH), BF16),
            vm((6 * W, 3 * CH), BF16),
            vm((6 * W, 3 * CH), BF16),
            vm((4 * W, LATENT), F32),
            vm((4 * W, LATENT), F32),
            vm((6 * W + 16, LATENT), F32),
            vm((4 * W, 3 * 384), BF16),
            vm((2 * W, CH), F32),
            vm((4 * W, 3 * LATENT), BF16),
            vm((2 * W, CH), F32),
            vm((8, 3 * JC, OWN), BF16),
            vm((JC, OWN), BF16),
            vm((JC, NB, CAP), BF16),
            vm((NB, JC, CAP), BF16),
            vm((NB, JC, CAP), BF16),
            vm((NB, 1, CAP), jnp.int32),
            vm((NB, 1, CAP), jnp.int32),
            vm((NB, LON, CAP), BF16),
            vm((NB, 1, CAP), F32),
            vm((NB, 1, CAP), F32),
            dma((2, 3)), dma((9,)), dma((9,)), dma((2, 8)), dma((2, 8)), dma((4, 2)), dma((4, 2)),
            dma((NB,)), dma((NB,)), dma((NB,)), dma((NB,)), dma, dma((NB,)), dma((NB,)),
        ],
        compiler_params=pltpu.CompilerParams(
            collective_id=0, has_side_effects=True, vmem_limit_bytes=60 * 1024 * 1024
        ),
    )(enc, dec, bias, x, seed, op, pos, live)


def local(
    analysed_fields,
    prediction_adjoint_seed,
    encoder_kernel_matrix,
    hidden_offset_term,
    decoder_kernel_matrix,
    measurement_wanted_positions,
    measurement_active_total,
    measurement_linear_operator,
):
    enc = jnp.transpose(encoder_kernel_matrix, (2, 3, 0, 1)).reshape(9, 64, FIELDS)
    dec = jnp.transpose(decoder_kernel_matrix, (2, 3, 1, 0)).reshape(9, 64, FIELDS)
    op = measurement_linear_operator[0, 0]
    sensitivity, imp = fused(
        enc, dec, hidden_offset_term[None], analysed_fields, prediction_adjoint_seed, op,
        measurement_wanted_positions[0, 0], measurement_active_total[0])
    return (sensitivity, imp[None, None])


def solution(mesh):
    in_specs = (
        P(None, "band", None),
        P(None, "band", None),
        P("chan", None, None, None),
        P("chan"),
        P(None, "chan", None, None),
        P("band", "chan", None, None),
        P("band", "chan", None),
        P("band", "chan", None, None, None),
    )
    out_specs = (P(None, "band", "chan"), P("band", "chan", None, None))
    return jax.shard_map(local, mesh=mesh, in_specs=in_specs, out_specs=out_specs, check_vma=False)
```
